512 devices in a mesh: pipe: 16 (over z_hi, y), expert: 32 (over z_lo, x, core).
Axes of the slice: x: 4, y: 4, z: 16 (z_hi: 4, z_lo: 4; z = z_hi * 4 + z_lo), core: 2. Of those that a mesh axis runs over, the one named last changes fastest.
Arguments:
- act_fwd: bfloat16 [16, 1024, 3584], P('pipe', 'expert'), may hold values from -6 to 6
- cot_bwd: bfloat16 [16, 1024, 3584], P('pipe', 'expert'), may hold values from -6 to 6
- routes_fwd: int32 [16, 1024, 2], P('pipe', 'expert'), may hold values from 0 to 3, all different within a row; in each aligned block of 32 rows (0 to 31, 32 to 63, ..., all dimensions but the last counted through in order) at most 18 rows name the same one
- gates_fwd: float32 [16, 1024, 2], P('pipe', 'expert'), may hold values from 0.1 to 1
- routes_bwd: int32 [16, 1024, 2], P('pipe', 'expert'), may hold values from 0 to 3, all different within a row; in each aligned block of 32 rows (0 to 31, 32 to 63, ..., all dimensions but the last counted through in order) at most 18 rows name the same one
- gates_bwd: float32 [16, 1024, 2], P('pipe', 'expert'), may hold values from 0.1 to 1
- w_in: bfloat16 [16, 2, 3584, 4096], P('pipe', None, None, 'expert'), may hold values from -0.09375 to 0.09375
- w_down: bfloat16 [16, 4096, 3584], P('pipe', 'expert'), may hold values from -0.1875 to 0.1875
- stash: bfloat16 [16, 18432, 128], P('pipe', 'expert'), may hold values from -0.59765625 to 0.59765625
Outputs:
- moe_out: bfloat16 [16, 1024, 3584], P('pipe', 'expert')
- grad_down: bfloat16 [16, 4096, 3584], P('pipe', 'expert')
The draws below stay inside these ranges and needn't reach their ends.
Inputs may be any that keep to these rules, and one draw needn't show every extreme that they name: `routes_fwd`: in the rows of one device no expert is named by more than 18 rows, a bound that some block reaches; a row names 2 different experts. `routes_bwd`: in the rows of one device no expert is named by more than 18 rows, a bound that some block reaches; a row names 2 different experts.
All inputs are finite; a program needn't handle non-finite values.
Results may differ from the reference program's by a relative error of at most 0.0059.
Values may be sent and summed in bfloat16 or wider, within the bound.
A program may use at most 128 MiB of HBM per device.

```python
import math
import jax
import jax.numpy as jnp
import numpy as np
from jax import lax

D = 3584
FF = 1024
EXPERTS = 4
TOP = 2
TOK_DEV = 32
CAP = 18
TOKENS = 1024
GROUP = 8
HDEV = 128
SLOTS = 576
N_PIPE = 16
N_EXPERT = 32


def block_levels(own_key, extent, shards, low, high):
    gain, own = 1.0, jax.random.fold_in(own_key, 6)
    for axis_at, shards_of in shards:
        heights = jnp.exp(jax.random.uniform(jax.random.fold_in(own, axis_at), (shards_of,), jnp.float32, low / len(shards), high / len(shards)))
        gain = gain * jnp.repeat(heights, extent[axis_at] // shards_of).reshape([-1 if axis == axis_at else 1 for axis in range(len(extent))])
    return gain


def shared_out(stream_key, own, number, rows, count, top, limit, skew):
    ranking = jax.random.permutation(stream_key, count)
    crowded, usual = portions_of(count, rows * top, limit, skew, True), portions_of(count, rows * top, limit, skew, False)
    places = jnp.arange(count)

    def named(lengths, rotation):
        used = int((lengths > 0).sum())
        fixed = max(1, used // 4)
        passed = fixed + (places - fixed + rotation * (used - fixed)) % max(1, count - fixed)
        return jnp.zeros((count,), jnp.int32).at[ranking[jnp.where(places < fixed, places, passed)]].set(jnp.asarray(lengths, jnp.int32))

    lengths = jnp.where(number % 4 == 0, named(crowded, number // 4), named(usual, number - number // 4 - 1))
    mixed = jax.random.permutation(jax.random.fold_in(own, 3), count)
    giver, taker = mixed[0:count // 2 * 2:2], mixed[1:count // 2 * 2:2]
    slack = jnp.minimum(lengths[giver] - 1, limit - lengths[taker]) // 2
    slack = jnp.where((giver == ranking[0]) | (taker == ranking[0]) | (lengths[taker] == 0), 0, jnp.maximum(slack, 0))
    passed = jax.random.randint(jax.random.fold_in(own, 4), (count // 2,), 0, 1 << 20) % (slack + 1)
    lengths = lengths.at[giver].add(-passed).at[taker].add(passed)
    items = jnp.searchsorted(jnp.cumsum(lengths), jnp.arange(rows * top), side="right").astype(jnp.int32)
    table = items.reshape(top, rows).T
    table = table[jax.random.permutation(jax.random.fold_in(own, 1), rows)]
    rotation = jax.random.randint(jax.random.fold_in(own, 2), (rows, 1), 0, top)
    return jnp.take_along_axis(table, (jnp.arange(top)[None, :] + rotation) % top, axis=1)


def portions_of(amount, total, bound, skew, full):
    weights = [(1 << 20) // math.isqrt(grade ** skew) + 1 for grade in range(1, amount + 1)]
    largest = bound if full else min(bound, max(-(-total // amount), total * weights[0] // sum(weights)))
    least = 1 if total - largest >= amount - 1 else 0
    given, surplus = [largest] + [least] * (amount - 1), total - largest - least * (amount - 1)
    while surplus > 0:
        movable = [i for i in range(1, amount) if given[i] < largest] or [i for i in range(1, amount) if given[i] < bound]
        mass, left = sum([weights[i] for i in movable]), surplus
        for i in movable:
            addition = min(bound - given[i], max(1, left * weights[i] // mass), surplus)
            given[i] = given[i] + addition
            surplus = surplus - addition
    return np.array(given)


def normal_values(stream_key, extent, spread, reach, cuts=(), held_as=jnp.bfloat16):
    level = block_levels(stream_key, extent, cuts, -0.22, 0.18) if cuts else 1.0
    array = jax.random.normal(stream_key, extent, jnp.float32) * spread * level
    return jnp.minimum(jnp.maximum(array, -reach), reach).astype(held_as)


def setup_inputs(seed: int = 0) -> dict:
    keys = jax.random.split(jax.random.key(seed), 10)
    act_fwd = normal_values(keys[0], (N_PIPE, TOKENS, D), 1.0, 6.0, ((0, 16), (1, 32)))
    cot_bwd = normal_values(keys[1], (N_PIPE, TOKENS, D), 1.0, 6.0, ((0, 16), (1, 32)))
    routes_fwd_keys = jax.random.split(jax.random.fold_in(keys[2], 1), N_PIPE * TOKENS // TOK_DEV)
    routes_fwd_turns = jax.random.permutation(jax.random.fold_in(keys[2], 3), N_PIPE * TOKENS // TOK_DEV)
    routes_fwd = jax.vmap(lambda own, number: shared_out(jax.random.fold_in(keys[2], 2), own, number, TOK_DEV, EXPERTS, TOP, CAP, 1))(routes_fwd_keys, routes_fwd_turns).reshape((N_PIPE, TOKENS, TOP))
    gates_fwd = jnp.clip(jnp.exp(math.log(1.0) - 2.3025851 * jax.random.uniform(keys[3], (N_PIPE, TOKENS, TOP), jnp.float32) ** block_levels(keys[3], (N_PIPE, TOKENS, TOP), ((0, 16), (1, 32)), -0.2, 0.2)), 0.1, 1.0)
    routes_bwd_keys = jax.random.split(jax.random.fold_in(keys[4], 1), N_PIPE * TOKENS // TOK_DEV)
    routes_bwd_turns = jax.random.permutation(jax.random.fold_in(keys[4], 3), N_PIPE * TOKENS // TOK_DEV)
    routes_bwd = jax.vmap(lambda own, number: shared_out(jax.random.fold_in(keys[4], 2), own, number, TOK_DEV, EXPERTS, TOP, CAP, 1))(routes_bwd_keys, routes_bwd_turns).reshape((N_PIPE, TOKENS, TOP))
    gates_bwd = jnp.clip(jnp.exp(math.log(1.0) - 2.3025851 * jax.random.uniform(keys[5], (N_PIPE, TOKENS, TOP), jnp.float32) ** block_levels(keys[5], (N_PIPE, TOKENS, TOP), ((0, 16), (1, 32)), -0.2, 0.2)), 0.1, 1.0)
    w_in = normal_values(keys[6], (N_PIPE, 2, D, EXPERTS * FF), D ** -0.5, 0.09375, ((0, 16), (3, 32)))
    w_down = normal_values(keys[7], (N_PIPE, EXPERTS * FF, D), FF ** -0.5, 0.1875, ((0, 16), (1, 32)))
    stash = normal_values(keys[8], (N_PIPE, N_EXPERT * SLOTS, HDEV), 0.1, 0.59765625, ((0, 16), (1, 32)))
    return dict(act_fwd=act_fwd, cot_bwd=cot_bwd, routes_fwd=routes_fwd, gates_fwd=gates_fwd, routes_bwd=routes_bwd, gates_bwd=gates_bwd, w_in=w_in, w_down=w_down, stash=stash)


def slot_table(routes):
    grouped = routes.reshape(N_EXPERT, TOK_DEV, TOP)
    hit_table = jnp.sum((grouped[..., None] == jnp.arange(EXPERTS, dtype=jnp.int32)).astype(jnp.int32), axis=2)
    position = (jnp.cumsum(hit_table, axis=1) - hit_table).astype(jnp.int32)
    slots = jnp.take_along_axis(position, grouped, axis=2).astype(jnp.int32)
    source = (jnp.arange(TOKENS, dtype=jnp.int32) // TOK_DEV)[:, None]
    return (source * CAP + slots.reshape(TOKENS, TOP)).astype(jnp.int32)


def expert_slots(routes, flat_slot, gates, expert_id):
    chosen = routes == expert_id
    where_slot = jnp.min(jnp.where(chosen, flat_slot, N_EXPERT * CAP), axis=1).astype(jnp.int32)
    weight = jnp.sum(jnp.where(chosen, gates, jnp.zeros_like(gates)), axis=1)
    return where_slot, weight


def forward_section(inputs, w_in_section, w_down_section, routes, gates):
    flat_slot = slot_table(routes)
    result = jnp.zeros((TOKENS, D), jnp.float32)
    for expert_id in range(EXPERTS):
        where_slot, weight = expert_slots(routes, flat_slot, gates, expert_id)
        buffer = jnp.zeros((N_EXPERT * CAP, D), jnp.bfloat16).at[where_slot].set(inputs, mode="drop")
        low = expert_id * FF
        gate_proj = jnp.dot(buffer, w_in_section[0, :, low:low + FF], preferred_element_type=jnp.float32)
        up_proj = jnp.dot(buffer, w_in_section[1, :, low:low + FF], preferred_element_type=jnp.float32)
        hidden = (jax.nn.silu(gate_proj) * up_proj).astype(jnp.bfloat16)
        summed = jnp.zeros((N_EXPERT * CAP, D), jnp.float32)
        for part_id in range(GROUP):
            start = part_id * HDEV
            partial_value = jnp.dot(hidden[:, start:start + HDEV], w_down_section[low + start:low + start + HDEV],
                              preferred_element_type=jnp.float32).astype(jnp.bfloat16)
            summed = summed + lax.optimization_barrier(partial_value).astype(jnp.float32)
        picked = summed[jnp.minimum(where_slot, N_EXPERT * CAP - 1)]
        result = result + weight[:, None] * picked
    return result.astype(jnp.bfloat16)


def backward_section(incoming, stash_section, routes, gates):
    flat_slot = slot_table(routes)
    pieces = []
    for expert_id in range(EXPERTS):
        where_slot, weight = expert_slots(routes, flat_slot, gates, expert_id)
        weighted = (weight[:, None] * incoming.astype(jnp.float32)).astype(jnp.bfloat16)
        buffer = jnp.zeros((N_EXPERT * CAP, D), jnp.bfloat16).at[where_slot].set(weighted, mode="drop")
        for part_id in range(GROUP):
            device = expert_id * GROUP + part_id
            stash_rows = stash_section[device * SLOTS:(device + 1) * SLOTS]
            pieces.append(jnp.dot(stash_rows.T, buffer, preferred_element_type=jnp.float32))
    return jnp.concatenate(pieces, axis=0)


def reference(act_fwd, cot_bwd, routes_fwd, gates_fwd, routes_bwd, gates_bwd, w_in, w_down, stash):
    inputs = jnp.roll(act_fwd, 1, axis=0)
    incoming_grad = jnp.roll(cot_bwd, -1, axis=0)
    moe_out = lax.map(lambda packed: forward_section(*packed), (inputs, w_in, w_down, routes_fwd, gates_fwd))
    local_grad = lax.map(lambda packed: backward_section(*packed), (incoming_grad, stash, routes_bwd, gates_bwd))
    rounded = lax.optimization_barrier(local_grad.astype(jnp.bfloat16)).astype(jnp.float32)
    grad_down = (rounded + jnp.flip(rounded, axis=0)).astype(jnp.bfloat16)
    return moe_out, grad_down
```

```python
import jax
import jax.numpy as jnp
from jax import lax
from jax.experimental import pallas as pl
from jax.experimental.pallas import tpu as pltpu
from jax.sharding import PartitionSpec as P

MESH = pl.DeviceIdType.MESH
EXPERTS = 4
CAP = 18
TOK = 32
D = 3584
HALF = 1792
QUART = 896
HID = 128
SLOTS = 576
BLOCK = 144
WIDE = 512
F32 = jnp.float32
BF16 = jnp.bfloat16


def iota(shape, axis):
    return lax.broadcasted_iota(jnp.int32, shape, axis)


def piece_width(k):
    return min(WIDE, HALF - k * WIDE)


def kernel(
    meta_ref, act_ref, cot_ref, win_ref, wdn_ref, stash_ref,
    moe_ref, grad_ref,
    meta_p, meta_c, meta_m,
    hop_f, hop_b, hop_m,
    sa_f, sa_b, sa_m, sl_f, sl_b, sl_m,
    lr_f, lr_b, lr_m, lr_r,
    x_f, x_b, x_m,
    win, wd, st, stm, sp32, spt, spmt,
    pre, pre_r, hid,
    po32, po, r_opp_l, r_opp_r, acc_r, acc_l, r_l, r_r,
    ret, ret_l, rows_r, mo, own_g, g,
    send_sem, recv_sem, local_sem,
):
    p = lax.axis_index("pipe")
    i = lax.axis_index("expert")
    n_pipe = lax.axis_size("pipe")
    c = lax.rem(i, 2)
    xq = lax.rem(lax.div(i, 2), 4)
    l = lax.div(i, 8)

    def at(pp, ll, xx, cc):
        return (pp, ll * 8 + xx * 2 + cc)

    nxt = lax.rem(p + 1, n_pipe)
    prv = lax.rem(p + n_pipe - 1, n_pipe)
    mirror = at(n_pipe - 1 - p, l, xq, c)
    partner = at(p, l, xq, 1 - c)
    right = at(p, l, lax.rem(xq + 1, 4), c)
    left = at(p, l, lax.rem(xq + 3, 4), c)

    def zdev(d):
        return lax.rem(l + d, 4)

    barrier = pltpu.get_barrier_semaphore()
    greeted = [at(q, l, xq, cc) for q in (nxt, prv) for cc in (c, 1 - c)]
    greeted += [at(p, zdev(d), xq, c) for d in (1, 2, 3)]
    greeted += [mirror, partner, right, left]
    for other in greeted:
        pl.semaphore_signal(barrier, inc=1, device_id=other, device_id_type=MESH)
    pl.semaphore_wait(barrier, len(greeted))

    used = [0, 0]
    sent = []
    local = []

    def remote(src, dst, device):
        k = used[0]
        used[0] += 1
        copy = pltpu.make_async_remote_copy(
            src_ref=src, dst_ref=dst, send_sem=send_sem.at[k], recv_sem=recv_sem.at[k],
            device_id=device, device_id_type=MESH,
        )
        copy.start()
        sent.append(copy)
        return copy

    def here(src, dst):
        k = used[1]
        used[1] += 1
        copy = pltpu.make_async_copy(src, dst, local_sem.at[k])
        copy.start()
        return copy

    def half_of(core):
        return pl.ds(pl.multiple_of(core * HALF, HALF), HALF)

    mine = pl.ds(pl.multiple_of(c * TOK, TOK), TOK)
    hops_f = []
    hops_b = []
    for d in (0, 1):
        core = lax.rem(c + d, 2)
        hops_f.append(remote(act_ref.at[0, :, half_of(core)], hop_f.at[mine], at(nxt, l, xq, core)))
        hops_b.append(remote(cot_ref.at[0, :, half_of(core)], hop_b.at[mine], at(prv, l, xq, core)))
    meta_copy = remote(meta_ref, meta_p, partner)
    stash_own = here(stash_ref.at[0], st.at[:, 0:HID])
    stash_other = remote(stash_ref.at[0], st.at[:, HID:2 * HID], partner)
    weights = []
    weights_other = []
    for s in (0, 1):
        weights.append(here(win_ref.at[0, s, half_of(c)], win.at[:, s * HID:(s + 1) * HID]))
        weights_other.append(
            remote(win_ref.at[0, s, half_of(1 - c)], win.at[:, (2 + s) * HID:(3 + s) * HID], partner)
        )
    weights.append(here(wdn_ref.at[0, :, half_of(c)], wd.at[0:HID]))
    weights_other.append(remote(wdn_ref.at[0, :, half_of(1 - c)], wd.at[HID:2 * HID], partner))

    meta_copy.wait_recv()
    meta_c[...] = meta_ref[...] + meta_p[...]

    def first_slots(meta, row):
        j = iota((32, 64), 0)
        lane = iota((32, 64), 1)
        core = (j >= CAP).astype(jnp.int32)
        wanted = (j - CAP * core + 1).astype(F32)
        same = (lane >= TOK).astype(jnp.int32) == core
        return [
            jnp.where((meta[row + e:row + e + 1, 0:64] == wanted) & same, 1.0, 0.0).astype(F32)
            for e in range(EXPERTS)
        ]

    def last_slots(meta, row, rows):
        r = iota((rows, 64), 0)
        lane = iota((rows, 64), 1)
        wanted = ((r & 3) + (32 - CAP + 1)).astype(F32)
        return [
            jnp.where((meta[row + e:row + e + 1, 0:64] == wanted) & (lane >= TOK), 1.0, 0.0).astype(F32)
            for e in range(EXPERTS)
        ]

    def chosen_rows(meta, row, weigh, hop, sa, sl):
        a = first_slots(meta, row)
        b = last_slots(meta, row, 16)
        sel_a = jnp.concatenate(a, axis=0)
        sel_b = jnp.concatenate(b, axis=0)
        if weigh:
            gates = [meta[row + 4 + e:row + 5 + e, 0:64] for e in range(EXPERTS)]
            gate_a = jnp.sum(jnp.concatenate([v * w for v, w in zip(a, gates)], axis=0), axis=1, keepdims=True)
            gate_b = jnp.sum(jnp.concatenate([v * w for v, w in zip(b, gates)], axis=0), axis=1, keepdims=True)
        sel_a = sel_a.astype(BF16)
        for t in range(7):
            cols = slice(t * 256, (t + 1) * 256)
            got = jnp.dot(sel_a, hop[:, cols], preferred_element_type=F32)
            if weigh:
                got = got * gate_a
            sa[:, cols] = got.astype(BF16)
        piece = (iota((64, 64), 0) >> 2) & 3
        parts = [jnp.where(piece == k, sel_b, 0.0).astype(BF16) for k in range(4)]
        for t in range(2):
            total = None
            for k in range(4):
                if t * 256 < piece_width(k):
                    low = k * WIDE + t * 256
                    got = jnp.dot(parts[k], hop[:, low:low + 256], preferred_element_type=F32)
                    total = got if total is None else total + got
            if weigh:
                total = total * gate_b
            sl[:, t * 256:(t + 1) * 256] = total.astype(BF16)

    rows_here = pl.ds(pl.multiple_of(l * 32, 32), 32)
    last_here = pl.ds(pl.multiple_of(l * 16, 16), 16)

    def exchange(sa, sl, rows, last):
        out = []
        for d in (2, 1, 3):
            e = zdev(d)
            device = at(p, e, xq, c)
            out.append(remote(sa.at[pl.ds(pl.multiple_of(e * 32, 32), 32)], rows.at[rows_here], device))
            out.append(remote(sl.at[pl.ds(pl.multiple_of(e * 16, 16), 16)], last.at[last_here], device))
        own = [here(sa.at[rows_here], rows.at[rows_here]), here(sl.at[last_here], last.at[last_here])]
        return out, own

    def arrived(copies):
        for copy in copies[0]:
            copy.wait_recv()
        for copy in copies[1]:
            copy.wait()

    def spread_last(last, rows):
        m = iota((16, 64), 0)
        n = iota((16, 64), 1)
        for k in range(4):
            width = piece_width(k)
            place = (m >> 2) * 16 + 4 * k + (m & 3)
            pick = jnp.where(n == place, 1.0, 0.0).astype(BF16)
            got = jnp.dot(pick, last[:, 0:width], preferred_element_type=F32)
            rows[128:BLOCK, k * WIDE:k * WIDE + width] = got.astype(BF16)

    def block(k):
        return slice(k * BLOCK, (k + 1) * BLOCK)

    A = slice(0, QUART)
    B = slice(QUART, HALF)

    def gather_start(x):
        ra = remote(x.at[block(0), A], x.at[block(1), A], right)
        lb = remote(x.at[block(0), B], x.at[block(2), B], left)
        rb = remote(x.at[block(0), B], x.at[block(1), B], right)
        la = remote(x.at[block(0), A], x.at[block(2), A], left)
        return [ra, lb, rb, la]

    def gather_forward(x, copies):
        copies[0].wait_recv()
        fr = remote(x.at[block(1), A], x.at[block(3), A], right)
        copies[1].wait_recv()
        fl = remote(x.at[block(2), B], x.at[block(3), B], left)
        return copies + [fr, fl]

    def permuted(source, target):
        for k, step in enumerate((0, 3, 1, 2)):
            m = iota((BLOCK, SLOTS), 0)
            n = iota((BLOCK, SLOTS), 1)
            at_x = lax.rem(xq + step, 4)
            early = (m >> 5) * BLOCK + (m & 31)
            late = ((m - 128) >> 2) * BLOCK + 32 + (m & 3)
            origin = jnp.where(m < 128, early, late) + at_x * 36
            pick = jnp.where(n == origin, 1.0, 0.0).astype(BF16)
            sp32[block(k)] = jnp.dot(pick, source[...], preferred_element_type=F32)
        target[...] = sp32[...].T.astype(BF16)

    stash_own.wait()
    stash_other.wait_recv()
    permuted(st, spt)

    for copy in hops_f:
        copy.wait_recv()
    chosen_rows(meta_c, 0, False, hop_f, sa_f, sl_f)
    to_f = exchange(sa_f, sl_f, x_f, lr_f)
    for copy in hops_b:
        copy.wait_recv()
    mirror_meta = remote(meta_c, meta_m, mirror)
    mirror_rows = remote(hop_b, hop_m, mirror)
    mirror_stash = remote(stash_ref.at[0], stm.at[:, 0:HID], mirror)
    chosen_rows(meta_c, 8, True, hop_b, sa_b, sl_b)
    to_b = exchange(sa_b, sl_b, x_b, lr_b)

    arrived(to_f)
    spread_last(lr_f, x_f)
    ag_f = gather_start(x_f)

    for copy in weights:
        copy.wait()
    for copy in weights_other:
        copy.wait_recv()

    def project(k):
        pre[block(k)] = jnp.dot(x_f[block(k)], win[...], preferred_element_type=F32)
        return remote(pre.at[block(k), 2 * HID:4 * HID], pre_r.at[block(k)], partner)

    def activate(k, copy):
        copy.wait_recv()
        gate = pre[block(k), 0:HID] + pre_r[block(k), 0:HID]
        up = pre[block(k), HID:2 * HID] + pre_r[block(k), HID:2 * HID]
        hid[block(k), 0:HID] = (gate / (1.0 + jnp.exp(-gate)) * up).astype(BF16)
        return remote(hid.at[block(k), 0:HID], hid.at[block(k), HID:2 * HID], partner)

    def down(k, copy):
        copy.wait_recv()

        @pl.loop(0, 7)
        def _(t):
            cols = pl.ds(pl.multiple_of(t * 256, 256), 256)
            got = jnp.dot(hid[block(k)], wd[:, cols], preferred_element_type=F32)
            po32[block(k), cols] = got
            po[block(k), cols] = got.astype(BF16)

    pre_0 = project(0)
    arrived(to_b)
    spread_last(lr_b, x_b)
    hid_0 = activate(0, pre_0)

    ag_f = gather_forward(x_f, ag_f)
    ag_b = gather_start(x_b)
    ag_f[2].wait_recv()
    ag_f[3].wait_recv()
    pre_1 = project(1)
    pre_2 = project(2)
    hid_1 = activate(1, pre_1)
    hid_2 = activate(2, pre_2)
    down(1, hid_1)
    to_left_a = remote(po.at[block(1), A], r_r.at[:, A], left)
    down(2, hid_2)
    to_right_b = remote(po.at[block(2), B], r_l.at[:, B], right)
    ag_f[4].wait_recv()
    ag_f[5].wait_recv()
    pre_3 = project(3)
    hid_3 = activate(3, pre_3)
    down(3, hid_3)
    opp_a = remote(po.at[block(3), A], r_opp_l, right)
    opp_b = remote(po.at[block(3), B], r_opp_r, left)
    down(0, hid_0)
    ag_b = gather_forward(x_b, ag_b)

    mirror_meta.wait_recv()
    mirror_rows.wait_recv()
    chosen_rows(meta_m, 8, True, hop_m, sa_m, sl_m)
    to_m = exchange(sa_m, sl_m, x_m, lr_m)
    mirror_stash.wait_recv()
    stash_pass = remote(stm.at[:, 0:HID], stm.at[:, HID:2 * HID], partner)

    opp_a.wait_recv()
    acc_r[...] = (po32[block(2), A] + r_opp_l[...].astype(F32)).astype(BF16)
    to_right_a = remote(acc_r, r_l.at[:, A], right)
    opp_b.wait_recv()
    acc_l[...] = (po32[block(1), B] + r_opp_r[...].astype(F32)).astype(BF16)
    to_left_b = remote(acc_l, r_r.at[:, B], left)

    arrived(to_m)
    spread_last(lr_m, x_m)
    ag_m = gather_start(x_m)

    stash_pass.wait_recv()
    permuted(stm, spmt)

    for copy in (to_right_a, to_right_b, to_left_a, to_left_b):
        copy.wait_recv()
    ret[...] = (po32[block(0)] + r_l[...].astype(F32) + r_r[...].astype(F32)).astype(BF16)
    m = iota((64, 16), 0)
    n = iota((64, 16), 1)
    place = (m >> 4) * 4 + (m & 3)
    for t in range(2):
        total = None
        for k in range(4):
            if t * 256 < piece_width(k):
                pick = jnp.where((n == place) & (((m >> 2) & 3) == k), 1.0, 0.0).astype(BF16)
                low = k * WIDE + t * 256
                got = jnp.dot(pick, ret[128:BLOCK, low:low + 256], preferred_element_type=F32)
                total = got if total is None else total + got
        ret_l[:, t * 256:(t + 1) * 256] = total.astype(BF16)
    to_r = exchange(ret, ret_l, rows_r, lr_r)

    ag_m = gather_forward(x_m, ag_m)
    for copy in ag_b[2:]:
        copy.wait_recv()

    @pl.loop(0, 7)
    def _(t):
        cols = pl.ds(pl.multiple_of(t * 256, 256), 256)
        own_g[:, cols] = jnp.dot(spt[...], x_b[:, cols], preferred_element_type=F32).astype(BF16)

    gates = [meta_c[4 + e:5 + e, 0:64] for e in range(EXPERTS)]
    table = [v * w for v, w in zip(first_slots(meta_c, 0), gates)]
    late = last_slots(meta_c, 0, 16)
    row = iota((16, 64), 0) >> 2
    tail = None
    for e in range(EXPERTS):
        part = jnp.where(row == e, late[e] * gates[e], 0.0)
        tail = part if tail is None else tail + part
    table = jnp.concatenate(table + [tail], axis=0).T
    table_hi = table.astype(BF16)
    table_lo = (table - table_hi.astype(F32)).astype(BF16)
    arrived(to_r)
    spread_last(lr_r, rows_r)
    for t in range(7):
        cols = slice(t * 256, (t + 1) * 256)
        got = jnp.dot(table_hi, rows_r[:, cols], preferred_element_type=F32)
        got += jnp.dot(table_lo, rows_r[:, cols], preferred_element_type=F32)
        mo[:, cols] = got.astype(BF16)
    theirs = pl.ds(pl.multiple_of((1 - c) * TOK, TOK), TOK)
    moe_other = remote(mo.at[theirs], moe_ref.at[0, :, half_of(c)], partner)
    moe_own = here(mo.at[mine], moe_ref.at[0, :, half_of(c)])

    for copy in ag_m[2:]:
        copy.wait_recv()

    @pl.loop(0, 7)
    def _(t):
        cols = pl.ds(pl.multiple_of(t * 256, 256), 256)
        other = jnp.dot(spmt[...], x_m[:, cols], preferred_element_type=F32).astype(BF16)
        g[:, cols] = (own_g[:, cols].astype(F32) + other.astype(F32)).astype(BF16)

    grad_other = remote(g.at[HID:2 * HID], grad_ref.at[0, :, half_of(c)], partner)
    grad_own = here(g.at[0:HID], grad_ref.at[0, :, half_of(c)])

    moe_own.wait()
    grad_own.wait()
    moe_other.wait_recv()
    grad_other.wait_recv()
    for copy in sent:
        copy.wait_send()


def slot_meta(routes, gates, core):
    ids = jnp.arange(EXPERTS, dtype=jnp.int32)
    match = routes[:, :, None] == ids
    hits = jnp.any(match, axis=1).astype(F32)
    weight = jnp.sum(jnp.where(match, gates[:, :, None], 0.0), axis=1)
    t = jnp.arange(TOK, dtype=jnp.int32)
    upto = (t[:, None] >= t[None, :]).astype(F32)
    count = jnp.sum(upto[:, :, None] * hits[None], axis=1)
    both = jnp.concatenate([(count * hits).T, weight.T], axis=0)
    lane_core = jnp.arange(128, dtype=jnp.int32) // TOK
    return jnp.where(lane_core[None, :] == core, jnp.tile(both, (1, 4)), 0.0)


def shards(act_fwd, cot_bwd, routes_fwd, gates_fwd, routes_bwd, gates_bwd, w_in, w_down, stash):
    core = lax.axis_index("expert") % 2
    meta = jnp.concatenate(
        [slot_meta(routes_fwd[0], gates_fwd[0], core), slot_meta(routes_bwd[0], gates_bwd[0], core)],
        axis=0,
    )
    V = pltpu.VMEM
    scratch = [
        V((16, 128), F32), V((16, 128), F32), V((16, 128), F32),
        V((64, HALF), BF16), V((64, HALF), BF16), V((64, HALF), BF16),
        V((128, HALF), BF16), V((128, HALF), BF16), V((128, HALF), BF16),
        V((64, WIDE), BF16), V((64, WIDE), BF16), V((64, WIDE), BF16),
        V((64, WIDE), BF16), V((64, WIDE), BF16), V((64, WIDE), BF16), V((64, WIDE), BF16),
        V((SLOTS, HALF), BF16), V((SLOTS, HALF), BF16), V((SLOTS, HALF), BF16),
        V((HALF, 4 * HID), BF16), V((2 * HID, HALF), BF16),
        V((SLOTS, 2 * HID), BF16), V((SLOTS, 2 * HID), BF16),
        V((SLOTS, 2 * HID), F32), V((2 * HID, SLOTS), BF16), V((2 * HID, SLOTS), BF16),
        V((SLOTS, 4 * HID), F32), V((SLOTS, 2 * HID), F32), V((SLOTS, 2 * HID), BF16),
        V((SLOTS, HALF), F32), V((SLOTS, HALF), BF16),
        V((BLOCK, QUART), BF16), V((BLOCK, QUART), BF16), V((BLOCK, QUART), BF16), V((BLOCK, QUART), BF16),
        V((BLOCK, HALF), BF16), V((BLOCK, HALF), BF16),
        V((BLOCK, HALF), BF16), V((64, WIDE), BF16), V((BLOCK, HALF), BF16),
        V((64, HALF), BF16), V((2 * HID, HALF), BF16), V((2 * HID, HALF), BF16),
        pltpu.SemaphoreType.DMA((80,)), pltpu.SemaphoreType.DMA((80,)), pltpu.SemaphoreType.DMA((24,)),
    ]
    anywhere = pl.BlockSpec(memory_space=pl.ANY)
    return pl.pallas_call(
        kernel,
        out_shape=(
            jax.ShapeDtypeStruct((1, TOK, D), BF16),
            jax.ShapeDtypeStruct((1, HID, D), BF16),
        ),
        in_specs=[pl.BlockSpec(memory_space=pltpu.VMEM)] + [anywhere] * 5,
        out_specs=(anywhere, anywhere),
        scratch_shapes=scratch,
        compiler_params=pltpu.CompilerParams(
            collective_id=0, has_side_effects=True, vmem_limit_bytes=50 * 1024 * 1024
        ),
    )(meta, act_fwd, cot_bwd, w_in, w_down, stash)


def solution(mesh):
    rows = P("pipe", "expert", None)
    in_specs = (rows, rows, rows, rows, rows, rows, P("pipe", None, None, "expert"), rows, rows)
    return jax.shard_map(shards, mesh=mesh, in_specs=in_specs, out_specs=(rows, rows), check_vma=False)
```

```python
import jax
import jax.numpy as jnp
from jax import lax
from jax.experimental import pallas as pl
from jax.experimental.pallas import tpu as pltpu
from jax.sharding import PartitionSpec as P

MESH = pl.DeviceIdType.MESH
EXPERTS = 4
CAP = 18
TOK = 32
D = 3584
HALF = 1792
QUART = 896
HID = 128
SLOTS = 576
BLOCK = 144
PIECE = 256
F32 = jnp.float32
BF16 = jnp.bfloat16


def iota(shape, axis):
    return lax.broadcasted_iota(jnp.int32, shape, axis)


def piece_width(k):
    return min(PIECE, QUART - k * PIECE)


def kernel(
    route_f_ref, gate_f_ref, route_b_ref, gate_b_ref, act_ref, cot_ref, win_ref, wdn_ref, stash_ref,
    moe_ref, grad_ref,
    meta_o, meta_p, meta_c, meta_m,
    hop_f, hop_b, hop_m, via_f1, via_f2, via_b1, via_b2,
    sa_f, sa_b, sa_m, sl_f, sl_b, sl_m,
    lr_f, lr_b, lr_m, lr_r,
    x_f, x_b, x_m,
    win, wd, st, stm, sp32, spt, spmt,
    pre, pre_r, hid,
    po32, po, r_opp_l, r_opp_r, acc_r, acc_l, r_l, r_r,
    ret, ret_l, rows_r, mo, own_g, g,
    send_sem, recv_sem, local_sem, hop_send, hop_recv,
):
    p = lax.axis_index("pipe")
    i = lax.axis_index("expert")
    n_pipe = lax.axis_size("pipe")
    c = lax.rem(i, 2)
    xq = lax.rem(lax.div(i, 2), 4)
    l = lax.div(i, 8)

    def at(pp, ll, xx, cc):
        return (pp, ll * 8 + xx * 2 + cc)

    y = lax.rem(p, 4)
    zh = lax.div(p, 4)
    n_zh = n_pipe // 4

    def section(yy, up):
        return lax.rem(zh + n_zh + up, n_zh) * 4 + yy

    mirror = at(n_pipe - 1 - p, l, xq, c)
    partner = at(p, l, xq, 1 - c)
    right = at(p, l, lax.rem(xq + 1, 4), c)
    left = at(p, l, lax.rem(xq + 3, 4), c)

    def zdev(d):
        return lax.rem(l + d, 4)

    barrier = pltpu.get_barrier_semaphore()
    greeted = [at(section(lax.rem(y + d, 4), 0), l, xq, cc) for d in (1, 2, 3) for cc in (c, 1 - c)]
    greeted += [at(section(y, up), l, xq, cc) for up in (1, -1) for cc in (c, 1 - c)]
    greeted += [at(p, zdev(d), xq, c) for d in (1, 2, 3)]
    greeted += [mirror, partner, right, left]
    for other in greeted:
        pl.semaphore_signal(barrier, inc=1, device_id=other, device_id_type=MESH)

    used = [0, 0]
    sent = []

    def remote(src, dst, device):
        k = used[0]
        used[0] += 1
        copy = pltpu.make_async_remote_copy(
            src_ref=src, dst_ref=dst, send_sem=send_sem.at[k], recv_sem=recv_sem.at[k],
            device_id=device, device_id_type=MESH,
        )
        copy.start()
        sent.append(copy)
        return copy

    def here(src, dst):
        k = used[1]
        used[1] += 1
        copy = pltpu.make_async_copy(src, dst, local_sem.at[k])
        copy.start()
        return copy

    def half_of(core):
        return pl.ds(pl.multiple_of(core * HALF, HALF), HALF)

    def quarter_of(core, q):
        return pl.ds(pl.multiple_of(core * HALF + q * QUART, 128), QUART)

    def cols_of(q):
        return slice(q * QUART, (q + 1) * QUART)

    A = cols_of(0)
    B = cols_of(1)
    mine = pl.ds(pl.multiple_of(c * TOK, TOK), TOK)

    def table_rows(routes, gates, row):
        e = iota((8, TOK), 0)
        first = routes[0:1] == e
        second = routes[1:2] == e
        hits = jnp.where(first | second, 1.0, 0.0).astype(F32)
        weight = jnp.where(first, gates[0:1], 0.0) + jnp.where(second, gates[1:2], 0.0)
        t = iota((TOK, 128), 0)
        lane = iota((TOK, 128), 1) - c * TOK
        upto = jnp.where((t <= lane) & (lane < TOK), 1.0, 0.0).astype(F32)
        place = jnp.where(t == lane, 1.0, 0.0).astype(F32)
        count = jnp.dot(hits, upto, preferred_element_type=F32)
        placed = jnp.dot(hits, place, preferred_element_type=F32)
        meta_o[row:row + 8] = count * placed
        meta_o[row + 8:row + 16] = jnp.dot(
            weight, place, precision=lax.Precision.HIGHEST, preferred_element_type=F32
        )

    table_rows(route_f_ref, gate_f_ref, 0)
    table_rows(route_b_ref, gate_b_ref, 16)
    weights = []
    for s in (0, 1):
        weights.append(here(win_ref.at[0, s, half_of(c)], win.at[:, s * HID:(s + 1) * HID]))
    weights.append(here(wdn_ref.at[0, :, half_of(c)], wd.at[0:HID]))
    stash_own = here(stash_ref.at[0], st.at[:, 0:HID])

    pl.semaphore_wait(barrier, len(greeted))

    def hop(k, src, dst, device, base):
        return pltpu.make_async_remote_copy(
            src_ref=src, dst_ref=dst, send_sem=hop_send.at[base + k], recv_sem=hop_recv.at[base + k],
            device_id=device, device_id_type=MESH,
        )

    class Stream:
        def __init__(self, src, rows, via_1, via_2, base, first, up, column):
            self.src, self.rows, self.via_1, self.via_2, self.base = src, rows, via_1, via_2, base
            self.up, self.column, self.ahead = up, column, up
            self.first = first
            self.last = 3 - first
            self.at_first = y == first
            self.at_last = y == self.last

        def piece(self, k):
            return self.src.at[0, :, pl.ds(pl.multiple_of(k * QUART, 128), QUART)]

        def final(self, src, core, q, device):
            cols = pl.ds(pl.multiple_of(q * QUART, 128), QUART)
            return hop(2 * q + lax.rem(c + core, 2), src, self.rows.at[mine, cols], device, self.base)

        def start(self):
            @pl.when(jnp.logical_not(self.at_last))
            def _():
                for q in (0, 1):
                    for d in (0, 1):
                        core = lax.rem(c + d, 2)
                        device = at(section(y + self.ahead, 0), l, xq, core)
                        self.final(self.piece(2 * core + q), core, q, device).start()

            @pl.when(self.at_last)
            def _():
                hop(5, self.piece(3), self.via_2, at(section(y, self.up), l, xq, c), self.base).start()
                for k in (1, 2, 0):
                    device = at(section(self.column(k), 0), l, xq, c)
                    pltpu.make_async_remote_copy(
                        src_ref=self.piece(k), dst_ref=self.via_1,
                        send_sem=hop_send.at[self.base + k], recv_sem=hop_recv.at[self.base + 4],
                        device_id=device, device_id_type=MESH,
                    ).start()

        def along_z(self):
            @pl.when(jnp.logical_not(self.at_last))
            def _():
                self.wait(4, self.via_1)

                @pl.when(self.at_first)
                def _():
                    device = at(section(y, self.up), l, xq, 0)
                    hop_to = self.rows.at[mine, A]
                    pltpu.make_async_remote_copy(
                        src_ref=self.via_1, dst_ref=hop_to, send_sem=hop_send.at[self.base + 5],
                        recv_sem=hop_recv.at[self.base + c],
                        device_id=device, device_id_type=MESH,
                    ).start()

                @pl.when(jnp.logical_not(self.at_first))
                def _():
                    hop(5, self.via_1, self.via_2, at(section(y, self.up), l, xq, c), self.base).start()

        def along_y(self):
            k = self.column(y)
            core = lax.div(k, 2)
            q = lax.rem(k, 2)
            self.wait(5, self.via_2)
            cols = pl.ds(pl.multiple_of(q * QUART, 128), QUART)
            pltpu.make_async_remote_copy(
                src_ref=self.via_2, dst_ref=self.rows.at[mine, cols], send_sem=hop_send.at[self.base + 4],
                recv_sem=hop_recv.at[self.base + 2 * q + lax.rem(c + core, 2)],
                device_id=at(section(self.first, 0), l, xq, core), device_id_type=MESH,
            ).start()

        def wait(self, k, ref):
            hop(k, ref, ref, partner, self.base).wait_recv()

        def arrived(self, q):
            for d in (0, 1):
                hop(2 * q + d, self.rows.at[mine, cols_of(q)], self.rows.at[mine, cols_of(q)], partner, self.base).wait_recv()

        def finish(self):
            for k in (0, 1, 2, 5):
                hop(k, self.via_1, self.via_1, partner, self.base).wait_send()

            @pl.when(jnp.logical_not(self.at_last))
            def _():
                hop(3, self.via_1, self.via_1, partner, self.base).wait_send()

            @pl.when(jnp.logical_not(self.at_first))
            def _():
                hop(4, self.via_2, self.via_2, partner, self.base).wait_send()

    stream_f = Stream(act_ref, hop_f, via_f1, via_f2, 0, 0, 1, lambda v: v)
    stream_b = Stream(cot_ref, hop_b, via_b1, via_b2, 6, 3, -1, lambda v: 3 - v)
    stream_f.start()
    stream_b.start()
    meta_copy = remote(meta_o, meta_p, partner)
    weights_other = []
    for s in (0, 1):
        weights_other.append(
            remote(win_ref.at[0, s, half_of(1 - c)], win.at[:, (2 + s) * HID:(3 + s) * HID], partner)
        )
    weights_other.append(remote(wdn_ref.at[0, :, half_of(1 - c)], wd.at[HID:2 * HID], partner))
    stash_other = remote(stash_ref.at[0], st.at[:, HID:2 * HID], partner)

    stream_f.along_z()
    stream_b.along_z()

    meta_copy.wait_recv()
    meta_c[...] = meta_o[...] + meta_p[...]

    def first_slots(meta, row):
        j = iota((32, 64), 0)
        lane = iota((32, 64), 1)
        core = (j >= CAP).astype(jnp.int32)
        wanted = (j - CAP * core + 1).astype(F32)
        same = (lane >= TOK).astype(jnp.int32) == core
        return [
            jnp.where((meta[row + e:row + e + 1, 0:64] == wanted) & same, 1.0, 0.0).astype(F32)
            for e in range(EXPERTS)
        ]

    def last_slots(meta, row, rows):
        r = iota((rows, 64), 0)
        lane = iota((rows, 64), 1)
        wanted = ((r & 3) + (32 - CAP + 1)).astype(F32)
        return [
            jnp.where((meta[row + e:row + e + 1, 0:64] == wanted) & (lane >= TOK), 1.0, 0.0).astype(F32)
            for e in range(EXPERTS)
        ]

    def selectors(meta, row, weigh):
        a = first_slots(meta, row)
        b = last_slots(meta, row, 16)
        sel_a = jnp.concatenate(a, axis=0)
        sel_b = jnp.concatenate(b, axis=0)
        gate_a = gate_b = None
        if weigh:
            gates = [meta[row + 8 + e:row + 9 + e, 0:64] for e in range(EXPERTS)]
            gate_a = jnp.sum(jnp.concatenate([v * w for v, w in zip(a, gates)], axis=0), axis=1, keepdims=True)
            gate_b = jnp.sum(jnp.concatenate([v * w for v, w in zip(b, gates)], axis=0), axis=1, keepdims=True)
        piece = (iota((64, 64), 0) >> 2) & 3
        parts = [jnp.where(piece == k, sel_b, 0.0).astype(BF16) for k in range(4)]
        return sel_a.astype(BF16), parts, gate_a, gate_b

    def chosen_rows(tables, q, hop, sa, sl):
        sel_a, parts, gate_a, gate_b = tables
        got = jnp.dot(sel_a, hop[:, cols_of(q)], preferred_element_type=F32)
        if gate_a is not None:
            got = got * gate_a
        sa[:, cols_of(q)] = got.astype(BF16)
        for t in range(2):
            total = None
            for k in range(4):
                if t * 128 < piece_width(k):
                    low = q * QUART + k * PIECE + t * 128
                    got = jnp.dot(parts[k], hop[:, low:low + 128], preferred_element_type=F32)
                    total = got if total is None else total + got
            if gate_b is not None:
                total = total * gate_b
            sl[:, q * PIECE + t * 128:q * PIECE + (t + 1) * 128] = total.astype(BF16)

    rows_here = pl.ds(pl.multiple_of(l * 32, 32), 32)
    last_here = pl.ds(pl.multiple_of(l * 16, 16), 16)

    def last_cols(q):
        return slice(q * PIECE, (q + 1) * PIECE)

    def exchange(q, sa, sl, rows, last):
        out = []
        for d in (2, 1, 3):
            e = zdev(d)
            device = at(p, e, xq, c)
            theirs = pl.ds(pl.multiple_of(e * 32, 32), 32)
            last_theirs = pl.ds(pl.multiple_of(e * 16, 16), 16)
            out.append(remote(sa.at[theirs, cols_of(q)], rows.at[rows_here, cols_of(q)], device))
            out.append(remote(sl.at[last_theirs, last_cols(q)], last.at[last_here, last_cols(q)], device))
        own = [
            here(sa.at[rows_here, cols_of(q)], rows.at[rows_here, cols_of(q)]),
            here(sl.at[last_here, last_cols(q)], last.at[last_here, last_cols(q)]),
        ]
        return out, own

    def arrived(copies):
        for copy in copies[0]:
            copy.wait_recv()
        for copy in copies[1]:
            copy.wait()

    def spread_last(q, last, rows):
        m = iota((16, 64), 0)
        n = iota((16, 64), 1)
        for k in range(4):
            width = piece_width(k)
            place = (m >> 2) * 16 + 4 * k + (m & 3)
            pick = jnp.where(n == place, 1.0, 0.0).astype(BF16)
            got = jnp.dot(pick, last[:, q * PIECE:q * PIECE + width], preferred_element_type=F32)
            low = q * QUART + k * PIECE
            rows[128:BLOCK, low:low + width] = got.astype(BF16)

    def block(k):
        return slice(k * BLOCK, (k + 1) * BLOCK)

    def gather_start(q, x):
        to_right = remote(x.at[block(0), cols_of(q)], x.at[block(1), cols_of(q)], right)
        to_left = remote(x.at[block(0), cols_of(q)], x.at[block(2), cols_of(q)], left)
        return [to_right, to_left]

    def gather_forward(q, x, copies):
        copies[q].wait_recv()
        if q == 0:
            return remote(x.at[block(1), A], x.at[block(3), A], right)
        return remote(x.at[block(2), B], x.at[block(3), B], left)

    def permuted(source, target):
        for k, step in enumerate((0, 3, 1, 2)):
            m = iota((BLOCK, SLOTS), 0)
            n = iota((BLOCK, SLOTS), 1)
            at_x = lax.rem(xq + step, 4)
            early = (m >> 5) * BLOCK + (m & 31)
            late = ((m - 128) >> 2) * BLOCK + 32 + (m & 3)
            origin = jnp.where(m < 128, early, late) + at_x * 36
            pick = jnp.where(n == origin, 1.0, 0.0).astype(BF16)
            sp32[block(k)] = jnp.dot(pick, source[...], preferred_element_type=F32)
        target[...] = sp32[...].T.astype(BF16)

    tables = selectors(meta_c, 0, False)
    to_f = []

    @pl.when(stream_f.at_first)
    def _():
        stream_b.along_y()

    for q in (0, 1):
        stream_f.arrived(q)
        chosen_rows(tables, q, hop_f, sa_f, sl_f)
        to_f.append(exchange(q, sa_f, sl_f, x_f, lr_f))

    @pl.when(jnp.logical_not(stream_f.at_first))
    def _():
        stream_f.along_y()

        @pl.when(jnp.logical_not(stream_b.at_first))
        def _():
            stream_b.along_y()

    mirror_meta = remote(meta_c, meta_m, mirror)
    mirror_rows = []
    tables = selectors(meta_c, 16, True)
    for q in (0, 1):
        stream_b.arrived(q)
        mirror_rows.append(remote(hop_b.at[:, cols_of(q)], hop_m.at[:, cols_of(q)], mirror))
        chosen_rows(tables, q, hop_b, sa_b, sl_b)

    ag_f = []
    arrived(to_f[0])
    spread_last(0, lr_f, x_f)
    ag_f.append(gather_start(0, x_f))
    to_b = [exchange(0, sa_b, sl_b, x_b, lr_b)]
    arrived(to_f[1])
    spread_last(1, lr_f, x_f)
    ag_f.append(gather_start(1, x_f))
    to_b.append(exchange(1, sa_b, sl_b, x_b, lr_b))

    for copy in weights:
        copy.wait()
    for copy in weights_other:
        copy.wait_recv()

    def project(k):
        pre[block(k)] = jnp.dot(x_f[block(k)], win[...], preferred_element_type=F32)
        return remote(pre.at[block(k), 2 * HID:4 * HID], pre_r.at[block(k)], partner)

    def activate(k, copy):
        copy.wait_recv()
        gate = pre[block(k), 0:HID] + pre_r[block(k), 0:HID]
        up = pre[block(k), HID:2 * HID] + pre_r[block(k), HID:2 * HID]
        hid[block(k), 0:HID] = (gate / (1.0 + jnp.exp(-gate)) * up).astype(BF16)
        return remote(hid.at[block(k), 0:HID], hid.at[block(k), HID:2 * HID], partner)

    def down(k, copy):
        copy.wait_recv()

        @pl.loop(0, 7)
        def _(t):
            cols = pl.ds(pl.multiple_of(t * 256, 256), 256)
            got = jnp.dot(hid[block(k)], wd[:, cols], preferred_element_type=F32)
            po32[block(k), cols] = got
            po[block(k), cols] = got.astype(BF16)

    pre_0 = project(0)
    ag_f.append(gather_forward(0, x_f, ag_f[0]))
    ag_f.append(gather_forward(1, x_f, ag_f[1]))
    hid_0 = activate(0, pre_0)
    stash_own.wait()
    stash_other.wait_recv()
    permuted(st, spt)

    ag_b = []
    for q in (0, 1):
        arrived(to_b[q])
        spread_last(q, lr_b, x_b)
        ag_b.append(gather_start(q, x_b))
    mirror_stash = remote(stash_ref.at[0], stm.at[:, 0:HID], mirror)

    ag_f[0][1].wait_recv()
    ag_f[1][0].wait_recv()
    pre_1 = project(1)
    pre_2 = project(2)
    hid_1 = activate(1, pre_1)
    hid_2 = activate(2, pre_2)
    down(1, hid_1)
    to_left_a = remote(po.at[block(1), A], r_r.at[:, A], left)
    down(2, hid_2)
    to_right_b = remote(po.at[block(2), B], r_l.at[:, B], right)
    ag_f[2].wait_recv()
    ag_f[3].wait_recv()
    pre_3 = project(3)
    hid_3 = activate(3, pre_3)
    down(3, hid_3)
    opp_a = remote(po.at[block(3), A], r_opp_l, right)
    opp_b = remote(po.at[block(3), B], r_opp_r, left)
    down(0, hid_0)

    mirror_meta.wait_recv()
    tables = selectors(meta_m, 16, True)
    to_m = []
    for q in (0, 1):
        mirror_rows[q].wait_recv()
        chosen_rows(tables, q, hop_m, sa_m, sl_m)
        to_m.append(exchange(q, sa_m, sl_m, x_m, lr_m))

    ag_b.append(gather_forward(0, x_b, ag_b[0]))
    ag_b.append(gather_forward(1, x_b, ag_b[1]))

    opp_a.wait_recv()
    acc_r[...] = (po32[block(2), A] + r_opp_l[...].astype(F32)).astype(BF16)
    to_right_a = remote(acc_r, r_l.at[:, A], right)
    opp_b.wait_recv()
    acc_l[...] = (po32[block(1), B] + r_opp_r[...].astype(F32)).astype(BF16)
    to_left_b = remote(acc_l, r_r.at[:, B], left)


    ag_m = []
    for q in (0, 1):
        arrived(to_m[q])
        spread_last(q, lr_m, x_m)
        ag_m.append(gather_start(q, x_m))

    to_r = []
    m = iota((64, 16), 0)
    n = iota((64, 16), 1)
    place = (m >> 4) * 4 + (m & 3)
    packs = [jnp.where((n == place) & (((m >> 2) & 3) == k), 1.0, 0.0).astype(BF16) for k in range(4)]
    for q, waited in ((0, (to_left_a, to_right_a)), (1, (to_right_b, to_left_b))):
        for copy in waited:
            copy.wait_recv()
        total = po32[block(0), cols_of(q)] + r_l[:, cols_of(q)].astype(F32) + r_r[:, cols_of(q)].astype(F32)
        ret[:, cols_of(q)] = total.astype(BF16)
        for t in range(2):
            total = None
            for k in range(4):
                if t * 128 < piece_width(k):
                    low = q * QUART + k * PIECE + t * 128
                    got = jnp.dot(packs[k], ret[128:BLOCK, low:low + 128], preferred_element_type=F32)
                    total = got if total is None else total + got
            ret_l[:, q * PIECE + t * 128:q * PIECE + (t + 1) * 128] = total.astype(BF16)
        to_r.append(exchange(q, ret, ret_l, rows_r, lr_r))

    mirror_stash.wait_recv()
    stash_pass = remote(stm.at[:, 0:HID], stm.at[:, HID:2 * HID], partner)
    stash_pass.wait_recv()
    permuted(stm, spmt)
    ag_m.append(gather_forward(0, x_m, ag_m[0]))
    ag_m.append(gather_forward(1, x_m, ag_m[1]))

    ag_b[0][1].wait_recv()
    ag_b[1][0].wait_recv()
    ag_b[2].wait_recv()
    ag_b[3].wait_recv()

    @pl.loop(0, 7)
    def _(t):
        cols = pl.ds(pl.multiple_of(t * 256, 256), 256)
        own_g[:, cols] = jnp.dot(spt[...], x_b[:, cols], preferred_element_type=F32).astype(BF16)

    gates = [meta_c[8 + e:9 + e, 0:64] for e in range(EXPERTS)]
    table = [v * w for v, w in zip(first_slots(meta_c, 0), gates)]
    late = last_slots(meta_c, 0, 16)
    row = iota((16, 64), 0) >> 2
    tail = None
    for e in range(EXPERTS):
        part = jnp.where(row == e, late[e] * gates[e], 0.0)
        tail = part if tail is None else tail + part
    table = jnp.concatenate(table + [tail], axis=0).T
    table_hi = table.astype(BF16)
    table_lo = (table - table_hi.astype(F32)).astype(BF16)
    theirs = pl.ds(pl.multiple_of((1 - c) * TOK, TOK), TOK)
    moe_other = []
    moe_own = []
    for q in (0, 1):
        arrived(to_r[q])
        spread_last(q, lr_r, rows_r)
        got = jnp.dot(table_hi, rows_r[:, cols_of(q)], preferred_element_type=F32)
        got += jnp.dot(table_lo, rows_r[:, cols_of(q)], preferred_element_type=F32)
        mo[:, cols_of(q)] = got.astype(BF16)
        moe_other.append(remote(mo.at[theirs, cols_of(q)], moe_ref.at[0, :, quarter_of(c, q)], partner))
        moe_own.append(here(mo.at[mine, cols_of(q)], moe_ref.at[0, :, quarter_of(c, q)]))

    ag_m[0][1].wait_recv()
    ag_m[1][0].wait_recv()
    ag_m[2].wait_recv()
    ag_m[3].wait_recv()

    @pl.loop(0, 7)
    def _(t):
        cols = pl.ds(pl.multiple_of(t * 256, 256), 256)
        other = jnp.dot(spmt[...], x_m[:, cols], preferred_element_type=F32).astype(BF16)
        g[:, cols] = (own_g[:, cols].astype(F32) + other.astype(F32)).astype(BF16)

    grad_other = remote(g.at[HID:2 * HID], grad_ref.at[0, :, half_of(c)], partner)
    grad_own = here(g.at[0:HID], grad_ref.at[0, :, half_of(c)])

    for copy in moe_own + [grad_own]:
        copy.wait()
    for copy in moe_other + [grad_other]:
        copy.wait_recv()
    for copy in sent:
        copy.wait_send()
    stream_f.finish()
    stream_b.finish()


def shards(act_fwd, cot_bwd, routes_fwd, gates_fwd, routes_bwd, gates_bwd, w_in, w_down, stash):
    V = pltpu.VMEM
    scratch = [
        V((32, 128), F32), V((32, 128), F32), V((32, 128), F32), V((32, 128), F32),
        V((64, HALF), BF16), V((64, HALF), BF16), V((64, HALF), BF16),
        V((TOK, QUART), BF16), V((TOK, QUART), BF16), V((TOK, QUART), BF16), V((TOK, QUART), BF16),
        V((128, HALF), BF16), V((128, HALF), BF16), V((128, HALF), BF16),
        V((64, 2 * PIECE), BF16), V((64, 2 * PIECE), BF16), V((64, 2 * PIECE), BF16),
        V((64, 2 * PIECE), BF16), V((64, 2 * PIECE), BF16), V((64, 2 * PIECE), BF16), V((64, 2 * PIECE), BF16),
        V((SLOTS, HALF), BF16), V((SLOTS, HALF), BF16), V((SLOTS, HALF), BF16),
        V((HALF, 4 * HID), BF16), V((2 * HID, HALF), BF16),
        V((SLOTS, 2 * HID), BF16), V((SLOTS, 2 * HID), BF16),
        V((SLOTS, 2 * HID), F32), V((2 * HID, SLOTS), BF16), V((2 * HID, SLOTS), BF16),
        V((SLOTS, 4 * HID), F32), V((SLOTS, 2 * HID), F32), V((SLOTS, 2 * HID), BF16),
        V((SLOTS, HALF), F32), V((SLOTS, HALF), BF16),
        V((BLOCK, QUART), BF16), V((BLOCK, QUART), BF16), V((BLOCK, QUART), BF16), V((BLOCK, QUART), BF16),
        V((BLOCK, HALF), BF16), V((BLOCK, HALF), BF16),
        V((BLOCK, HALF), BF16), V((64, 2 * PIECE), BF16), V((BLOCK, HALF), BF16),
        V((64, HALF), BF16), V((2 * HID, HALF), BF16), V((2 * HID, HALF), BF16),
        pltpu.SemaphoreType.DMA((128,)), pltpu.SemaphoreType.DMA((128,)), pltpu.SemaphoreType.DMA((32,)),
        pltpu.SemaphoreType.DMA((12,)), pltpu.SemaphoreType.DMA((12,)),
    ]
    hbm = pl.BlockSpec(memory_space=pltpu.HBM)
    return pl.pallas_call(
        kernel,
        out_shape=(
            jax.ShapeDtypeStruct((1, TOK, D), BF16),
            jax.ShapeDtypeStruct((1, HID, D), BF16),
        ),
        in_specs=[pl.BlockSpec(memory_space=pltpu.VMEM)] * 4 + [hbm] * 5,
        out_specs=(hbm, hbm),
        scratch_shapes=scratch,
        compiler_params=pltpu.CompilerParams(
            collective_id=0, has_side_effects=True, vmem_limit_bytes=56 * 1024 * 1024
        ),
    )(
        routes_fwd[0].T, gates_fwd[0].T, routes_bwd[0].T, gates_bwd[0].T,
        act_fwd, cot_bwd, w_in, w_down, stash,
    )


def solution(mesh):
    rows = P("pipe", "expert", None)
    in_specs = (rows, rows, rows, rows, rows, rows, P("pipe", None, None, "expert"), rows, rows)
    return jax.shard_map(shards, mesh=mesh, in_specs=in_specs, out_specs=(rows, rows), check_vma=False)
```

```python
import jax
import jax.numpy as jnp
from jax import lax
from jax.experimental import pallas as pl
from jax.experimental.pallas import tpu as pltpu
from jax.sharding import PartitionSpec as P

MESH = pl.DeviceIdType.MESH
EXPERTS = 4
CAP = 18
TOK = 32
D = 3584
HALF = 1792
QUART = 896
HID = 128
SLOTS = 576
BLOCK = 144
PIECE = 256
F32 = jnp.float32
BF16 = jnp.bfloat16


def iota(shape, axis):
    return lax.broadcasted_iota(jnp.int32, shape, axis)


def piece_width(k):
    return min(PIECE, QUART - k * PIECE)


def kernel(
    route_f_ref, gate_f_ref, route_b_ref, gate_b_ref, act_ref, cot_ref, win_ref, wdn_ref, stash_ref,
    moe_ref, grad_ref,
    meta_o, meta_p, meta_c, meta_m,
    hop_f, hop_b, hop_m, via_f1, via_f2, via_b1, via_b2,
    sa_f, sa_b, sa_m, sl_f, sl_b, sl_m,
    lr_f, lr_b, lr_m, lr_r,
    x_f, x_b, x_m,
    win, wd, st, stm, sp32, spt, spmt, spm_last,
    pre, pre_r, hid,
    po32, po, r_opp_l, r_opp_r, acc_r, acc_l, r_l, r_r,
    ret, ret_l, rows_r, mo, own_g, g,
    send_sem, recv_sem, local_sem, hop_send, hop_recv,
):
    p = lax.axis_index("pipe")
    i = lax.axis_index("expert")
    n_pipe = lax.axis_size("pipe")
    c = lax.rem(i, 2)
    xq = lax.rem(lax.div(i, 2), 4)
    l = lax.div(i, 8)

    def at(pp, ll, xx, cc):
        return (pp, ll * 8 + xx * 2 + cc)

    y = lax.rem(p, 4)
    zh = lax.div(p, 4)
    n_zh = n_pipe // 4

    def section(yy, up):
        return lax.rem(zh + n_zh + up, n_zh) * 4 + yy

    mirror = at(n_pipe - 1 - p, l, xq, c)
    partner = at(p, l, xq, 1 - c)
    right = at(p, l, lax.rem(xq + 1, 4), c)
    left = at(p, l, lax.rem(xq + 3, 4), c)

    def zdev(d):
        return lax.rem(l + d, 4)

    barrier = pltpu.get_barrier_semaphore()
    greeted = [at(section(lax.rem(y + d, 4), 0), l, xq, cc) for d in (1, 2, 3) for cc in (c, 1 - c)]
    greeted += [at(section(y, up), l, xq, cc) for up in (1, -1) for cc in (c, 1 - c)]
    greeted += [at(p, zdev(d), xq, c) for d in (1, 2, 3)]
    greeted += [mirror, partner, right, left]
    for other in greeted:
        pl.semaphore_signal(barrier, inc=1, device_id=other, device_id_type=MESH)

    used = [0, 0]
    sent = []

    def remote(src, dst, device):
        k = used[0]
        used[0] += 1
        copy = pltpu.make_async_remote_copy(
            src_ref=src, dst_ref=dst, send_sem=send_sem.at[k], recv_sem=recv_sem.at[k],
            device_id=device, device_id_type=MESH,
        )
        copy.start()
        sent.append(copy)
        return copy

    def here(src, dst):
        k = used[1]
        used[1] += 1
        copy = pltpu.make_async_copy(src, dst, local_sem.at[k])
        copy.start()
        return copy

    def half_of(core):
        return pl.ds(pl.multiple_of(core * HALF, HALF), HALF)

    def quarter_of(core, q):
        return pl.ds(pl.multiple_of(core * HALF + q * QUART, 128), QUART)

    def cols_of(q):
        return slice(q * QUART, (q + 1) * QUART)

    A = cols_of(0)
    B = cols_of(1)
    mine = pl.ds(pl.multiple_of(c * TOK, TOK), TOK)

    def table_rows(routes, gates, row):
        e = iota((8, TOK), 0)
        first = routes[0:1] == e
        second = routes[1:2] == e
        hits = jnp.where(first | second, 1.0, 0.0).astype(F32)
        weight = jnp.where(first, gates[0:1], 0.0) + jnp.where(second, gates[1:2], 0.0)
        t = iota((TOK, 128), 0)
        lane = iota((TOK, 128), 1) - c * TOK
        upto = jnp.where((t <= lane) & (lane < TOK), 1.0, 0.0).astype(F32)
        place = jnp.where(t == lane, 1.0, 0.0).astype(F32)
        count = jnp.dot(hits, upto, preferred_element_type=F32)
        placed = jnp.dot(hits, place, preferred_element_type=F32)
        meta_o[row:row + 8] = count * placed
        meta_o[row + 8:row + 16] = jnp.dot(
            weight, place, precision=lax.Precision.HIGHEST, preferred_element_type=F32
        )

    pl.semaphore_wait(barrier, len(greeted))

    def hop(k, src, dst, device, base):
        return pltpu.make_async_remote_copy(
            src_ref=src, dst_ref=dst, send_sem=hop_send.at[base + k], recv_sem=hop_recv.at[base + k],
            device_id=device, device_id_type=MESH,
        )

    class Stream:
        def __init__(self, src, rows, via_1, via_2, base, first, up, column):
            self.src, self.rows, self.via_1, self.via_2, self.base = src, rows, via_1, via_2, base
            self.up, self.column, self.ahead = up, column, up
            self.first = first
            self.last = 3 - first
            self.at_first = y == first
            self.at_last = y == self.last

        def piece(self, k):
            return self.src.at[0, :, pl.ds(pl.multiple_of(k * QUART, 128), QUART)]

        def final(self, src, core, q, device):
            cols = pl.ds(pl.multiple_of(q * QUART, 128), QUART)
            return hop(2 * q + lax.rem(c + core, 2), src, self.rows.at[mine, cols], device, self.base)

        def start(self):
            @pl.when(jnp.logical_not(self.at_last))
            def _():
                for q in (0, 1):
                    for d in (0, 1):
                        core = lax.rem(c + d, 2)
                        device = at(section(y + self.ahead, 0), l, xq, core)
                        self.final(self.piece(2 * core + q), core, q, device).start()

            @pl.when(self.at_last)
            def _():
                hop(5, self.piece(3), self.via_2, at(section(y, self.up), l, xq, c), self.base).start()
                for k in (1, 2, 0):
                    device = at(section(self.column(k), 0), l, xq, c)
                    pltpu.make_async_remote_copy(
                        src_ref=self.piece(k), dst_ref=self.via_1,
                        send_sem=hop_send.at[self.base + k], recv_sem=hop_recv.at[self.base + 4],
                        device_id=device, device_id_type=MESH,
                    ).start()

        def along_z(self):
            @pl.when(jnp.logical_not(self.at_last))
            def _():
                self.wait(4, self.via_1)

                @pl.when(self.at_first)
                def _():
                    device = at(section(y, self.up), l, xq, 0)
                    hop_to = self.rows.at[mine, A]
                    pltpu.make_async_remote_copy(
                        src_ref=self.via_1, dst_ref=hop_to, send_sem=hop_send.at[self.base + 5],
                        recv_sem=hop_recv.at[self.base + c],
                        device_id=device, device_id_type=MESH,
                    ).start()

                @pl.when(jnp.logical_not(self.at_first))
                def _():
                    hop(5, self.via_1, self.via_2, at(section(y, self.up), l, xq, c), self.base).start()

        def along_y(self):
            k = self.column(y)
            core = lax.div(k, 2)
            q = lax.rem(k, 2)
            self.wait(5, self.via_2)
            cols = pl.ds(pl.multiple_of(q * QUART, 128), QUART)
            pltpu.make_async_remote_copy(
                src_ref=self.via_2, dst_ref=self.rows.at[mine, cols], send_sem=hop_send.at[self.base + 4],
                recv_sem=hop_recv.at[self.base + 2 * q + lax.rem(c + core, 2)],
                device_id=at(section(self.first, 0), l, xq, core), device_id_type=MESH,
            ).start()

        def wait(self, k, ref):
            hop(k, ref, ref, partner, self.base).wait_recv()

        def arrived(self, q):
            for d in (0, 1):
                hop(2 * q + d, self.rows.at[mine, cols_of(q)], self.rows.at[mine, cols_of(q)], partner, self.base).wait_recv()

        def finish(self):
            for k in (0, 1, 2, 5):
                hop(k, self.via_1, self.via_1, partner, self.base).wait_send()

            @pl.when(jnp.logical_not(self.at_last))
            def _():
                hop(3, self.via_1, self.via_1, partner, self.base).wait_send()

            @pl.when(jnp.logical_not(self.at_first))
            def _():
                hop(4, self.via_2, self.via_2, partner, self.base).wait_send()

    stream_f = Stream(act_ref, hop_f, via_f1, via_f2, 0, 0, 1, lambda v: v)
    stream_b = Stream(cot_ref, hop_b, via_b1, via_b2, 6, 3, -1, lambda v: 3 - v)
    stream_f.start()
    stream_b.start()
    table_rows(route_f_ref, gate_f_ref, 0)
    table_rows(route_b_ref, gate_b_ref, 16)
    weights = []
    for s in (0, 1):
        weights.append(here(win_ref.at[0, s, half_of(c)], win.at[:, s * HID:(s + 1) * HID]))
    weights.append(here(wdn_ref.at[0, :, half_of(c)], wd.at[0:HID]))
    stash_own = here(stash_ref.at[0], st.at[:, 0:HID])
    meta_copy = remote(meta_o, meta_p, partner)
    weights_other = []
    for s in (0, 1):
        weights_other.append(
            remote(win_ref.at[0, s, half_of(1 - c)], win.at[:, (2 + s) * HID:(3 + s) * HID], partner)
        )
    weights_other.append(remote(wdn_ref.at[0, :, half_of(1 - c)], wd.at[HID:2 * HID], partner))
    stash_other = remote(stash_ref.at[0], st.at[:, HID:2 * HID], partner)

    stream_f.along_z()
    stream_b.along_z()

    meta_copy.wait_recv()
    meta_c[...] = meta_o[...] + meta_p[...]

    def first_slots(meta, row):
        j = iota((32, 64), 0)
        lane = iota((32, 64), 1)
        core = (j >= CAP).astype(jnp.int32)
        wanted = (j - CAP * core + 1).astype(F32)
        same = (lane >= TOK).astype(jnp.int32) == core
        return [
            jnp.where((meta[row + e:row + e + 1, 0:64] == wanted) & same, 1.0, 0.0).astype(F32)
            for e in range(EXPERTS)
        ]

    def last_slots(meta, row, rows):
        r = iota((rows, 64), 0)
        lane = iota((rows, 64), 1)
        wanted = ((r & 3) + (32 - CAP + 1)).astype(F32)
        return [
            jnp.where((meta[row + e:row + e + 1, 0:64] == wanted) & (lane >= TOK), 1.0, 0.0).astype(F32)
            for e in range(EXPERTS)
        ]

    def selectors(meta, row, weigh):
        a = first_slots(meta, row)
        b = last_slots(meta, row, 16)
        sel_a = jnp.concatenate(a, axis=0)
        sel_b = jnp.concatenate(b, axis=0)
        gate_a = gate_b = None
        if weigh:
            gates = [meta[row + 8 + e:row + 9 + e, 0:64] for e in range(EXPERTS)]
            gate_a = jnp.sum(jnp.concatenate([v * w for v, w in zip(a, gates)], axis=0), axis=1, keepdims=True)
            gate_b = jnp.sum(jnp.concatenate([v * w for v, w in zip(b, gates)], axis=0), axis=1, keepdims=True)
        piece = (iota((64, 64), 0) >> 2) & 3
        parts = [jnp.where(piece == k, sel_b, 0.0).astype(BF16) for k in range(4)]
        return sel_a.astype(BF16), parts, gate_a, gate_b

    def chosen_rows(tables, q, hop, sa, sl):
        sel_a, parts, gate_a, gate_b = tables
        got = jnp.dot(sel_a, hop[:, cols_of(q)], preferred_element_type=F32)
        if gate_a is not None:
            got = got * gate_a
        sa[:, cols_of(q)] = got.astype(BF16)
        for t in range(2):
            total = None
            for k in range(4):
                if t * 128 < piece_width(k):
                    low = q * QUART + k * PIECE + t * 128
                    got = jnp.dot(parts[k], hop[:, low:low + 128], preferred_element_type=F32)
                    total = got if total is None else total + got
            if gate_b is not None:
                total = total * gate_b
            sl[:, q * PIECE + t * 128:q * PIECE + (t + 1) * 128] = total.astype(BF16)

    rows_here = pl.ds(pl.multiple_of(l * 32, 32), 32)
    last_here = pl.ds(pl.multiple_of(l * 16, 16), 16)

    def last_cols(q):
        return slice(q * PIECE, (q + 1) * PIECE)

    def exchange(q, sa, sl, rows, last):
        out = []
        for d in (2, 1, 3):
            e = zdev(d)
            device = at(p, e, xq, c)
            k = 4 - d
            theirs = pl.ds(pl.multiple_of(e * 32, 32), 32)
            last_theirs = pl.ds(pl.multiple_of(e * 16, 16), 16)
            out.append(remote(sa.at[theirs, cols_of(q)], rows.at[k * 32:(k + 1) * 32, cols_of(q)], device))
            out.append(remote(sl.at[last_theirs, last_cols(q)], last.at[k * 16:(k + 1) * 16, last_cols(q)], device))
        own = [
            here(sa.at[rows_here, cols_of(q)], rows.at[0:32, cols_of(q)]),
            here(sl.at[last_here, last_cols(q)], last.at[0:16, last_cols(q)]),
        ]
        return out, own

    def exchange_back(q, rows, last, back, back_last):
        out = []
        for d in (2, 1, 3):
            device = at(p, zdev(d), xq, c)
            out.append(remote(rows.at[d * 32:(d + 1) * 32, cols_of(q)], back.at[rows_here, cols_of(q)], device))
            out.append(remote(last.at[d * 16:(d + 1) * 16, last_cols(q)], back_last.at[last_here, last_cols(q)], device))
        own = [
            here(rows.at[0:32, cols_of(q)], back.at[rows_here, cols_of(q)]),
            here(last.at[0:16, last_cols(q)], back_last.at[last_here, last_cols(q)]),
        ]
        return out, own

    def arrived(copies):
        for copy in copies[0]:
            copy.wait_recv()
        for copy in copies[1]:
            copy.wait()

    def spread_last(q, last, rows):
        m = iota((16, 64), 0)
        n = iota((16, 64), 1)
        for k in range(4):
            width = piece_width(k)
            place = (m >> 2) * 16 + 4 * k + (m & 3)
            pick = jnp.where(n == place, 1.0, 0.0).astype(BF16)
            got = jnp.dot(pick, last[:, q * PIECE:q * PIECE + width], preferred_element_type=F32)
            low = q * QUART + k * PIECE
            rows[128:BLOCK, low:low + width] = got.astype(BF16)

    def block(k):
        return slice(k * BLOCK, (k + 1) * BLOCK)

    def part(k, n):
        return slice(k * BLOCK, k * BLOCK + 32) if n == 0 else slice(k * BLOCK + 32, (k + 1) * BLOCK)

    class Gather:
        def __init__(self, x, sa):
            self.x, self.sa = x, sa
            self.copies = {}

        def start(self, n, q):
            x = self.x
            src = self.sa.at[rows_here, cols_of(q)] if n == 0 else x.at[part(0, 1), cols_of(q)]
            sides = [(1, right), (2, left)]
            for k, device in sides if q == 0 else sides[::-1]:
                self.copies[n, q, k] = remote(src, x.at[part(k, n), cols_of(q)], device)

        def forward(self, n):
            x = self.x
            for q, k, device in ((0, 1, right), (1, 2, left)):
                self.copies[n, q, k].wait_recv()
                self.copies[n, q, 3] = remote(x.at[part(k, n), cols_of(q)], x.at[part(3, n), cols_of(q)], device)

        def near(self):
            for n in (0, 1):
                self.copies[n, 0, 2].wait_recv()
                self.copies[n, 1, 1].wait_recv()

        def far(self, *halves):
            for q in halves or (0, 1):
                self.copies[0, q, 3].wait_recv()
                self.copies[1, q, 3].wait_recv()

    def permuted(source, target, last=None):
        for k, step in enumerate((0, 3, 1, 2)):
            m = iota((BLOCK, SLOTS), 0)
            n = iota((BLOCK, SLOTS), 1)
            at_x = lax.rem(xq + step, 4)
            early = ((l + (m >> 5)) & 3) * BLOCK + (m & 31)
            late = ((l + ((m - 128) >> 2)) & 3) * BLOCK + 32 + (m & 3)
            origin = jnp.where(m < 128, early, late) + at_x * 36
            pick = jnp.where(n == origin, 1.0, 0.0).astype(BF16)
            sp32[block(k)] = jnp.dot(pick, source[...], preferred_element_type=F32)
        target[...] = sp32[...].T.astype(BF16)
        if last is not None:
            last[...] = sp32[block(3)].T.astype(BF16)

    tables = selectors(meta_c, 0, False)
    to_f = []
    ag_f = Gather(x_f, sa_f)
    ag_b = Gather(x_b, sa_b)
    ag_m = Gather(x_m, sa_m)

    @pl.when(stream_f.at_first)
    def _():
        stream_b.along_y()

    for q in (0, 1):
        stream_f.arrived(q)
        chosen_rows(tables, q, hop_f, sa_f, sl_f)
        to_f.append(exchange(q, sa_f, sl_f, x_f, lr_f))
        ag_f.start(0, q)

    @pl.when(jnp.logical_not(stream_f.at_first))
    def _():
        stream_f.along_y()

        @pl.when(jnp.logical_not(stream_b.at_first))
        def _():
            stream_b.along_y()

    tables = selectors(meta_c, 16, True)
    for q in (0, 1):
        stream_b.arrived(q)
        chosen_rows(tables, q, hop_b, sa_b, sl_b)
        ag_b.start(0, q)

    ag_f.forward(0)
    to_b = []
    for q in (0, 1):
        arrived(to_f[q])
        spread_last(q, lr_f, x_f)
        ag_f.start(1, q)
        to_b.append(exchange(q, sa_b, sl_b, x_b, lr_b))
    ag_b.forward(0)

    for copy in weights:
        copy.wait()
    for copy in weights_other:
        copy.wait_recv()

    def blocks(k, n):
        return slice(k * BLOCK, (k + n) * BLOCK)

    def project(k, n):
        rows = blocks(k, n)
        pre[rows] = jnp.dot(x_f[rows], win[...], preferred_element_type=F32)
        return remote(pre.at[rows, 2 * HID:4 * HID], pre_r.at[rows], partner)

    def activate(k, n, copy):
        rows = blocks(k, n)
        copy.wait_recv()
        gate = pre[rows, 0:HID] + pre_r[rows, 0:HID]
        up = pre[rows, HID:2 * HID] + pre_r[rows, HID:2 * HID]
        hid[rows, 0:HID] = (gate / (1.0 + jnp.exp(-gate)) * up).astype(BF16)
        return remote(hid.at[rows, 0:HID], hid.at[rows, HID:2 * HID], partner)

    def down(k, n):
        rows = blocks(k, n)

        @pl.loop(0, 7)
        def _(t):
            cols = pl.ds(pl.multiple_of(t * 256, 256), 256)
            got = jnp.dot(hid[rows], wd[:, cols], preferred_element_type=F32)
            po32[rows, cols] = got
            po[rows, cols] = got.astype(BF16)

    mirror_meta = remote(meta_c, meta_m, mirror)
    mirror_rows = [remote(hop_b.at[:, cols_of(q)], hop_m.at[:, cols_of(q)], mirror) for q in (0, 1)]
    pre_0 = project(0, 1)
    ag_f.forward(1)
    hid_0 = activate(0, 1, pre_0)
    stash_own.wait()
    stash_other.wait_recv()
    permuted(st, spt)

    for q in (0, 1):
        arrived(to_b[q])
        spread_last(q, lr_b, x_b)
        ag_b.start(1, q)

    ag_f.near()
    pre_1 = project(1, 2)
    hid_1 = activate(1, 2, pre_1)
    hid_1.wait_recv()
    down(1, 2)
    to_left_a = remote(po.at[block(1), A], r_r.at[:, A], left)
    to_right_b = remote(po.at[block(2), B], r_l.at[:, B], right)
    ag_f.far()
    pre_3 = project(3, 1)
    hid_3 = activate(3, 1, pre_3)
    hid_3.wait_recv()
    down(3, 1)
    opp_a = remote(po.at[block(3), A], r_opp_l, right)
    opp_b = remote(po.at[block(3), B], r_opp_r, left)
    hid_0.wait_recv()
    down(0, 1)

    mirror_meta.wait_recv()
    tables = selectors(meta_m, 16, True)
    to_m = []
    for q in (0, 1):
        mirror_rows[q].wait_recv()
        chosen_rows(tables, q, hop_m, sa_m, sl_m)
        to_m.append(exchange(q, sa_m, sl_m, x_m, lr_m))
        ag_m.start(0, q)

    mirror_stash = remote(stash_ref.at[0], stm.at[:, 0:HID], mirror)
    opp_a.wait_recv()
    acc_r[...] = (po32[block(2), A] + r_opp_l[...].astype(F32)).astype(BF16)
    to_right_a = remote(acc_r, r_l.at[:, A], right)
    opp_b.wait_recv()
    acc_l[...] = (po32[block(1), B] + r_opp_r[...].astype(F32)).astype(BF16)
    to_left_b = remote(acc_l, r_r.at[:, B], left)
    ag_b.forward(1)


    to_r = []
    m = iota((64, 16), 0)
    n = iota((64, 16), 1)
    place = (m >> 4) * 4 + (m & 3)
    packs = [jnp.where((n == place) & (((m >> 2) & 3) == k), 1.0, 0.0).astype(BF16) for k in range(4)]
    for q, waited in ((0, (to_left_a, to_right_a)), (1, (to_right_b, to_left_b))):
        for copy in waited:
            copy.wait_recv()
        total = po32[block(0), cols_of(q)] + r_l[:, cols_of(q)].astype(F32) + r_r[:, cols_of(q)].astype(F32)
        ret[:, cols_of(q)] = total.astype(BF16)
        for t in range(2):
            total = None
            for k in range(4):
                if t * 128 < piece_width(k):
                    low = q * QUART + k * PIECE + t * 128
                    got = jnp.dot(packs[k], ret[128:BLOCK, low:low + 128], preferred_element_type=F32)
                    total = got if total is None else total + got
            ret_l[:, q * PIECE + t * 128:q * PIECE + (t + 1) * 128] = total.astype(BF16)
        to_r.append(exchange_back(q, ret, ret_l, rows_r, lr_r))

    ag_m.forward(0)
    for q in (0, 1):
        arrived(to_m[q])
        spread_last(q, lr_m, x_m)
        ag_m.start(1, q)
    ag_m.forward(1)
    mirror_stash.wait_recv()
    stash_pass = remote(stm.at[:, 0:HID], stm.at[:, HID:2 * HID], partner)

    ag_b.near()
    ag_b.far()

    @pl.loop(0, 7)
    def _(t):
        cols = pl.ds(pl.multiple_of(t * 256, 256), 256)
        own_g[:, cols] = jnp.dot(spt[...], x_b[:, cols], preferred_element_type=F32).astype(BF16)

    stash_pass.wait_recv()
    permuted(stm, spmt, spm_last)
    gates = [meta_c[8 + e:9 + e, 0:64] for e in range(EXPERTS)]
    table = [v * w for v, w in zip(first_slots(meta_c, 0), gates)]
    late = last_slots(meta_c, 0, 16)
    row = iota((16, 64), 0) >> 2
    tail = None
    for e in range(EXPERTS):
        part = jnp.where(row == e, late[e] * gates[e], 0.0)
        tail = part if tail is None else tail + part
    table = jnp.concatenate(table + [tail], axis=0).T
    table_hi = table.astype(BF16)
    table_lo = (table - table_hi.astype(F32)).astype(BF16)
    theirs = pl.ds(pl.multiple_of((1 - c) * TOK, TOK), TOK)
    moe_other = []
    moe_own = []
    for q in (0, 1):
        arrived(to_r[q])
        spread_last(q, lr_r, rows_r)
        got = jnp.dot(table_hi, rows_r[:, cols_of(q)], preferred_element_type=F32)
        got += jnp.dot(table_lo, rows_r[:, cols_of(q)], preferred_element_type=F32)
        mo[:, cols_of(q)] = got.astype(BF16)
        moe_other.append(remote(mo.at[theirs, cols_of(q)], moe_ref.at[0, :, quarter_of(c, q)], partner))
        moe_own.append(here(mo.at[mine, cols_of(q)], moe_ref.at[0, :, quarter_of(c, q)]))

    ag_m.near()

    @pl.loop(0, 7)
    def _(t):
        cols = pl.ds(pl.multiple_of(t * 256, 256), 256)
        po32[0:256, cols] = jnp.dot(
            spmt[:, 0:3 * BLOCK], x_m[0:3 * BLOCK, cols], preferred_element_type=F32
        )

    grads = []
    for q in (0, 1):
        ag_m.far(q)

        @pl.loop(0, 7)
        def _(t):
            cols = pl.ds(pl.multiple_of(q * QUART + t * 128, 128), 128)
            other = jnp.dot(spm_last[...], x_m[block(3), cols], preferred_element_type=F32)
            other = (po32[0:256, cols] + other).astype(BF16)
            g[:, cols] = (own_g[:, cols].astype(F32) + other.astype(F32)).astype(BF16)

        there = grad_ref.at[0, :, quarter_of(c, q)]
        grads.append((remote(g.at[HID:2 * HID, cols_of(q)], there, partner), here(g.at[0:HID, cols_of(q)], there)))

    for copy in moe_own:
        copy.wait()
    for copy in moe_other:
        copy.wait_recv()
    for other, own in grads:
        own.wait()
        other.wait_recv()
    for copy in sent:
        copy.wait_send()
    stream_f.finish()
    stream_b.finish()


def shards(act_fwd, cot_bwd, routes_fwd, gates_fwd, routes_bwd, gates_bwd, w_in, w_down, stash):
    V = pltpu.VMEM
    scratch = [
        V((32, 128), F32), V((32, 128), F32), V((32, 128), F32), V((32, 128), F32),
        V((64, HALF), BF16), V((64, HALF), BF16), V((64, HALF), BF16),
        V((TOK, QUART), BF16), V((TOK, QUART), BF16), V((TOK, QUART), BF16), V((TOK, QUART), BF16),
        V((128, HALF), BF16), V((128, HALF), BF16), V((128, HALF), BF16),
        V((64, 2 * PIECE), BF16), V((64, 2 * PIECE), BF16), V((64, 2 * PIECE), BF16),
        V((64, 2 * PIECE), BF16), V((64, 2 * PIECE), BF16), V((64, 2 * PIECE), BF16), V((64, 2 * PIECE), BF16),
        V((SLOTS, HALF), BF16), V((SLOTS, HALF), BF16), V((SLOTS, HALF), BF16),
        V((HALF, 4 * HID), BF16), V((2 * HID, HALF), BF16),
        V((SLOTS, 2 * HID), BF16), V((SLOTS, 2 * HID), BF16),
        V((SLOTS, 2 * HID), F32), V((2 * HID, SLOTS), BF16), V((2 * HID, SLOTS), BF16), V((2 * HID, BLOCK), BF16),
        V((SLOTS, 4 * HID), F32), V((SLOTS, 2 * HID), F32), V((SLOTS, 2 * HID), BF16),
        V((SLOTS, HALF), F32), V((SLOTS, HALF), BF16),
        V((BLOCK, QUART), BF16), V((BLOCK, QUART), BF16), V((BLOCK, QUART), BF16), V((BLOCK, QUART), BF16),
        V((BLOCK, HALF), BF16), V((BLOCK, HALF), BF16),
        V((BLOCK, HALF), BF16), V((64, 2 * PIECE), BF16), V((BLOCK, HALF), BF16),
        V((64, HALF), BF16), V((2 * HID, HALF), BF16), V((2 * HID, HALF), BF16),
        pltpu.SemaphoreType.DMA((128,)), pltpu.SemaphoreType.DMA((128,)), pltpu.SemaphoreType.DMA((32,)),
        pltpu.SemaphoreType.DMA((12,)), pltpu.SemaphoreType.DMA((12,)),
    ]
    hbm = pl.BlockSpec(memory_space=pltpu.HBM)
    return pl.pallas_call(
        kernel,
        out_shape=(
            jax.ShapeDtypeStruct((1, TOK, D), BF16),
            jax.ShapeDtypeStruct((1, HID, D), BF16),
        ),
        in_specs=[pl.BlockSpec(memory_space=pltpu.VMEM)] * 4 + [hbm] * 5,
        out_specs=(hbm, hbm),
        scratch_shapes=scratch,
        compiler_params=pltpu.CompilerParams(
            collective_id=0, has_side_effects=True, vmem_limit_bytes=56 * 1024 * 1024
        ),
    )(
        routes_fwd[0].T, gates_fwd[0].T, routes_bwd[0].T, gates_bwd[0].T,
        act_fwd, cot_bwd, w_in, w_down, stash,
    )


def solution(mesh):
    rows = P("pipe", "expert", None)
    in_specs = (rows, rows, rows, rows, rows, rows, P("pipe", None, None, "expert"), rows, rows)
    return jax.shard_map(shards, mesh=mesh, in_specs=in_specs, out_specs=(rows, rows), check_vma=False)
```

```python
import jax
import jax.numpy as jnp
from jax import lax
from jax.experimental import pallas as pl
from jax.experimental.pallas import tpu as pltpu
from jax.sharding import PartitionSpec as P

MESH = pl.DeviceIdType.MESH
EXPERTS = 4
CAP = 18
TOK = 32
D = 3584
HALF = 1792
QUART = 896
HID = 128
SLOTS = 576
BLOCK = 144
PIECE = 256
F32 = jnp.float32
BF16 = jnp.bfloat16


def iota(shape, axis):
    return lax.broadcasted_iota(jnp.int32, shape, axis)


def piece_width(k):
    return min(PIECE, QUART - k * PIECE)


def kernel(
    route_f_ref, gate_f_ref, route_b_ref, gate_b_ref, act_ref, cot_ref, win_ref, wdn_ref, stash_ref,
    moe_ref, grad_ref,
    route_f, gate_f, route_b, gate_b, meta_o, meta_p, meta_c, meta_m,
    hop_f, hop_b, hop_m, via_f1, via_f2, via_b1, via_b2,
    sa_f, sa_b, sa_m, sl_f, sl_b, sl_m,
    lr_f, lr_b, lr_m, lr_r,
    x_f, x_b, x_m,
    win, wd, st, stm, sp32, spt, spmt, spm_last,
    pre, pre_r, hid,
    po32, po, r_opp_l, r_opp_r, acc_r, acc_l, r_l, r_r,
    ret, ret_l, rows_r, mo, own_g, g,
    send_sem, recv_sem, local_sem, hop_send, hop_recv, small_sem,
):
    p = lax.axis_index("pipe")
    i = lax.axis_index("expert")
    n_pipe = lax.axis_size("pipe")
    c = lax.rem(i, 2)
    xq = lax.rem(lax.div(i, 2), 4)
    l = lax.div(i, 8)

    def at(pp, ll, xx, cc):
        return (pp, ll * 8 + xx * 2 + cc)

    y = lax.rem(p, 4)
    zh = lax.div(p, 4)
    n_zh = n_pipe // 4

    def section(yy, up):
        return lax.rem(zh + n_zh + up, n_zh) * 4 + yy

    mirror = at(n_pipe - 1 - p, l, xq, c)
    partner = at(p, l, xq, 1 - c)
    right = at(p, l, lax.rem(xq + 1, 4), c)
    left = at(p, l, lax.rem(xq + 3, 4), c)

    def zdev(d):
        return lax.rem(l + d, 4)

    small = [(route_f_ref, route_f), (gate_f_ref, gate_f), (route_b_ref, route_b), (gate_b_ref, gate_b)]
    small = [pltpu.make_async_copy(src, dst, small_sem.at[k]) for k, (src, dst) in enumerate(small)]
    for copy in small:
        copy.start()
    barrier = pltpu.get_barrier_semaphore()
    greeted = [at(section(lax.rem(y + d, 4), 0), l, xq, cc) for d in (1, 2, 3) for cc in (c, 1 - c)]
    greeted += [at(section(y, up), l, xq, cc) for up in (1, -1) for cc in (c, 1 - c)]
    greeted += [at(p, zdev(d), xq, c) for d in (1, 2, 3)]
    greeted += [mirror, partner, right, left]
    for other in greeted:
        pl.semaphore_signal(barrier, inc=1, device_id=other, device_id_type=MESH)

    used = [0, 0]
    sent = []

    def remote(src, dst, device):
        k = used[0]
        used[0] += 1
        copy = pltpu.make_async_remote_copy(
            src_ref=src, dst_ref=dst, send_sem=send_sem.at[k], recv_sem=recv_sem.at[k],
            device_id=device, device_id_type=MESH,
        )
        copy.start()
        sent.append(copy)
        return copy

    def here(src, dst):
        k = used[1]
        used[1] += 1
        copy = pltpu.make_async_copy(src, dst, local_sem.at[k])
        copy.start()
        return copy

    def half_of(core):
        return pl.ds(pl.multiple_of(core * HALF, HALF), HALF)

    def quarter_of(core, q):
        return pl.ds(pl.multiple_of(core * HALF + q * QUART, 128), QUART)

    def cols_of(q):
        return slice(q * QUART, (q + 1) * QUART)

    A = cols_of(0)
    B = cols_of(1)
    mine = pl.ds(pl.multiple_of(c * TOK, TOK), TOK)

    def table_rows(routes, gates, row):
        e = iota((8, TOK), 0)
        first = routes[0:1] == e
        second = routes[1:2] == e
        hits = jnp.where(first | second, 1.0, 0.0).astype(F32)
        weight = jnp.where(first, gates[0:1], 0.0) + jnp.where(second, gates[1:2], 0.0)
        t = iota((TOK, 128), 0)
        lane = iota((TOK, 128), 1) - c * TOK
        upto = jnp.where((t <= lane) & (lane < TOK), 1.0, 0.0).astype(F32)
        place = jnp.where(t == lane, 1.0, 0.0).astype(F32)
        count = jnp.dot(hits, upto, preferred_element_type=F32)
        placed = jnp.dot(hits, place, preferred_element_type=F32)
        meta_o[row:row + 8] = count * placed
        meta_o[row + 8:row + 16] = jnp.dot(
            weight, place, precision=lax.Precision.HIGHEST, preferred_element_type=F32
        )

    pl.semaphore_wait(barrier, len(greeted))

    def hop(k, src, dst, device, base):
        return pltpu.make_async_remote_copy(
            src_ref=src, dst_ref=dst, send_sem=hop_send.at[base + k], recv_sem=hop_recv.at[base + k],
            device_id=device, device_id_type=MESH,
        )

    class Stream:
        def __init__(self, src, rows, via_1, via_2, base, first, up, column):
            self.src, self.rows, self.via_1, self.via_2, self.base = src, rows, via_1, via_2, base
            self.up, self.column, self.ahead = up, column, up
            self.first = first
            self.last = 3 - first
            self.at_first = y == first
            self.at_last = y == self.last

        def piece(self, k):
            return self.src.at[0, :, pl.ds(pl.multiple_of(k * QUART, 128), QUART)]

        def final(self, src, core, q, device):
            cols = pl.ds(pl.multiple_of(q * QUART, 128), QUART)
            return hop(2 * q + lax.rem(c + core, 2), src, self.rows.at[mine, cols], device, self.base)

        def start(self):
            @pl.when(jnp.logical_not(self.at_last))
            def _():
                for q in (0, 1):
                    for d in (0, 1):
                        core = lax.rem(c + d, 2)
                        device = at(section(y + self.ahead, 0), l, xq, core)
                        self.final(self.piece(2 * core + q), core, q, device).start()

            @pl.when(self.at_last)
            def _():
                hop(5, self.piece(3), self.via_2, at(section(y, self.up), l, xq, c), self.base).start()
                for k in (1, 2, 0):
                    device = at(section(self.column(k), 0), l, xq, c)
                    pltpu.make_async_remote_copy(
                        src_ref=self.piece(k), dst_ref=self.via_1,
                        send_sem=hop_send.at[self.base + k], recv_sem=hop_recv.at[self.base + 4],
                        device_id=device, device_id_type=MESH,
                    ).start()

        def along_z(self):
            @pl.when(jnp.logical_not(self.at_last))
            def _():
                self.wait(4, self.via_1)

                @pl.when(self.at_first)
                def _():
                    device = at(section(y, self.up), l, xq, 0)
                    hop_to = self.rows.at[mine, A]
                    pltpu.make_async_remote_copy(
                        src_ref=self.via_1, dst_ref=hop_to, send_sem=hop_send.at[self.base + 5],
                        recv_sem=hop_recv.at[self.base + c],
                        device_id=device, device_id_type=MESH,
                    ).start()

                @pl.when(jnp.logical_not(self.at_first))
                def _():
                    hop(5, self.via_1, self.via_2, at(section(y, self.up), l, xq, c), self.base).start()

        def along_y(self):
            k = self.column(y)
            core = lax.div(k, 2)
            q = lax.rem(k, 2)
            self.wait(5, self.via_2)
            cols = pl.ds(pl.multiple_of(q * QUART, 128), QUART)
            pltpu.make_async_remote_copy(
                src_ref=self.via_2, dst_ref=self.rows.at[mine, cols], send_sem=hop_send.at[self.base + 4],
                recv_sem=hop_recv.at[self.base + 2 * q + lax.rem(c + core, 2)],
                device_id=at(section(self.first, 0), l, xq, core), device_id_type=MESH,
            ).start()

        def wait(self, k, ref):
            hop(k, ref, ref, partner, self.base).wait_recv()

        def arrived(self, q):
            for d in (0, 1):
                hop(2 * q + d, self.rows.at[mine, cols_of(q)], self.rows.at[mine, cols_of(q)], partner, self.base).wait_recv()

        def finish(self):
            for k in (0, 1, 2, 5):
                hop(k, self.via_1, self.via_1, partner, self.base).wait_send()

            @pl.when(jnp.logical_not(self.at_last))
            def _():
                hop(3, self.via_1, self.via_1, partner, self.base).wait_send()

            @pl.when(jnp.logical_not(self.at_first))
            def _():
                hop(4, self.via_2, self.via_2, partner, self.base).wait_send()

    stream_f = Stream(act_ref, hop_f, via_f1, via_f2, 0, 0, 1, lambda v: v)
    stream_b = Stream(cot_ref, hop_b, via_b1, via_b2, 6, 3, -1, lambda v: 3 - v)
    stream_f.start()
    stream_b.start()
    for copy in small:
        copy.wait()
    table_rows(route_f, gate_f, 0)
    table_rows(route_b, gate_b, 16)
    weights = []
    for s in (0, 1):
        weights.append(here(win_ref.at[0, s, half_of(c)], win.at[:, s * HID:(s + 1) * HID]))
    weights.append(here(wdn_ref.at[0, :, half_of(c)], wd.at[0:HID]))
    stash_own = here(stash_ref.at[0], st.at[:, 0:HID])
    meta_copy = remote(meta_o, meta_p, partner)
    weights_other = []
    for s in (0, 1):
        weights_other.append(
            remote(win_ref.at[0, s, half_of(1 - c)], win.at[:, (2 + s) * HID:(3 + s) * HID], partner)
        )
    weights_other.append(remote(wdn_ref.at[0, :, half_of(1 - c)], wd.at[HID:2 * HID], partner))
    stash_other = remote(stash_ref.at[0], st.at[:, HID:2 * HID], partner)

    stream_f.along_z()
    stream_b.along_z()

    meta_copy.wait_recv()
    meta_c[...] = meta_o[...] + meta_p[...]

    def first_slots(meta, row):
        j = iota((32, 64), 0)
        lane = iota((32, 64), 1)
        core = (j >= CAP).astype(jnp.int32)
        wanted = (j - CAP * core + 1).astype(F32)
        same = (lane >= TOK).astype(jnp.int32) == core
        return [
            jnp.where((meta[row + e:row + e + 1, 0:64] == wanted) & same, 1.0, 0.0).astype(F32)
            for e in range(EXPERTS)
        ]

    def last_slots(meta, row, rows):
        r = iota((rows, 64), 0)
        lane = iota((rows, 64), 1)
        wanted = ((r & 3) + (32 - CAP + 1)).astype(F32)
        return [
            jnp.where((meta[row + e:row + e + 1, 0:64] == wanted) & (lane >= TOK), 1.0, 0.0).astype(F32)
            for e in range(EXPERTS)
        ]

    def selectors(meta, row, weigh):
        a = first_slots(meta, row)
        b = last_slots(meta, row, 16)
        sel_a = jnp.concatenate(a, axis=0)
        sel_b = jnp.concatenate(b, axis=0)
        gate_a = gate_b = None
        if weigh:
            gates = [meta[row + 8 + e:row + 9 + e, 0:64] for e in range(EXPERTS)]
            gate_a = jnp.sum(jnp.concatenate([v * w for v, w in zip(a, gates)], axis=0), axis=1, keepdims=True)
            gate_b = jnp.sum(jnp.concatenate([v * w for v, w in zip(b, gates)], axis=0), axis=1, keepdims=True)
        piece = (iota((64, 64), 0) >> 2) & 3
        parts = [jnp.where(piece == k, sel_b, 0.0).astype(BF16) for k in range(4)]
        return sel_a.astype(BF16), parts, gate_a, gate_b

    def chosen_rows(tables, q, hop, sa, sl):
        sel_a, parts, gate_a, gate_b = tables
        got = jnp.dot(sel_a, hop[:, cols_of(q)], preferred_element_type=F32)
        if gate_a is not None:
            got = got * gate_a
        sa[:, cols_of(q)] = got.astype(BF16)
        for t in range(2):
            total = None
            for k in range(4):
                if t * 128 < piece_width(k):
                    low = q * QUART + k * PIECE + t * 128
                    got = jnp.dot(parts[k], hop[:, low:low + 128], preferred_element_type=F32)
                    total = got if total is None else total + got
            if gate_b is not None:
                total = total * gate_b
            sl[:, q * PIECE + t * 128:q * PIECE + (t + 1) * 128] = total.astype(BF16)

    rows_here = pl.ds(pl.multiple_of(l * 32, 32), 32)
    last_here = pl.ds(pl.multiple_of(l * 16, 16), 16)

    def last_cols(q):
        return slice(q * PIECE, (q + 1) * PIECE)

    def exchange(q, sa, sl, rows, last):
        out = []
        for d in (2, 1, 3):
            e = zdev(d)
            device = at(p, e, xq, c)
            k = 4 - d
            theirs = pl.ds(pl.multiple_of(e * 32, 32), 32)
            last_theirs = pl.ds(pl.multiple_of(e * 16, 16), 16)
            out.append(remote(sa.at[theirs, cols_of(q)], rows.at[k * 32:(k + 1) * 32, cols_of(q)], device))
            out.append(remote(sl.at[last_theirs, last_cols(q)], last.at[k * 16:(k + 1) * 16, last_cols(q)], device))
        own = [
            here(sa.at[rows_here, cols_of(q)], rows.at[0:32, cols_of(q)]),
            here(sl.at[last_here, last_cols(q)], last.at[0:16, last_cols(q)]),
        ]
        return out, own

    def exchange_back(q, rows, last, back, back_last):
        out = []
        for d in (2, 1, 3):
            device = at(p, zdev(d), xq, c)
            out.append(remote(rows.at[d * 32:(d + 1) * 32, cols_of(q)], back.at[rows_here, cols_of(q)], device))
            out.append(remote(last.at[d * 16:(d + 1) * 16, last_cols(q)], back_last.at[last_here, last_cols(q)], device))
        own = [
            here(rows.at[0:32, cols_of(q)], back.at[rows_here, cols_of(q)]),
            here(last.at[0:16, last_cols(q)], back_last.at[last_here, last_cols(q)]),
        ]
        return out, own

    def arrived(copies):
        for copy in copies[0]:
            copy.wait_recv()
        for copy in copies[1]:
            copy.wait()

    def spread_last(q, last, rows):
        m = iota((16, 64), 0)
        n = iota((16, 64), 1)
        for k in range(4):
            width = piece_width(k)
            place = (m >> 2) * 16 + 4 * k + (m & 3)
            pick = jnp.where(n == place, 1.0, 0.0).astype(BF16)
            got = jnp.dot(pick, last[:, q * PIECE:q * PIECE + width], preferred_element_type=F32)
            low = q * QUART + k * PIECE
            rows[128:BLOCK, low:low + width] = got.astype(BF16)

    def block(k):
        return slice(k * BLOCK, (k + 1) * BLOCK)

    def part(k, n):
        return slice(k * BLOCK, k * BLOCK + 32) if n == 0 else slice(k * BLOCK + 32, (k + 1) * BLOCK)

    class Gather:
        def __init__(self, x, sa):
            self.x, self.sa = x, sa
            self.copies = {}

        def start(self, n, q):
            x = self.x
            src = self.sa.at[rows_here, cols_of(q)] if n == 0 else x.at[part(0, 1), cols_of(q)]
            sides = [(1, right), (2, left)]
            for k, device in sides if q == 0 else sides[::-1]:
                self.copies[n, q, k] = remote(src, x.at[part(k, n), cols_of(q)], device)

        def forward(self, n):
            x = self.x
            for q, k, device in ((0, 1, right), (1, 2, left)):
                self.copies[n, q, k].wait_recv()
                self.copies[n, q, 3] = remote(x.at[part(k, n), cols_of(q)], x.at[part(3, n), cols_of(q)], device)

        def near(self):
            for n in (0, 1):
                self.copies[n, 0, 2].wait_recv()
                self.copies[n, 1, 1].wait_recv()

        def far(self, *halves):
            for q in halves or (0, 1):
                self.copies[0, q, 3].wait_recv()
                self.copies[1, q, 3].wait_recv()

    def permuted(source, target, last=None):
        for k, step in enumerate((0, 3, 1, 2)):
            m = iota((BLOCK, SLOTS), 0)
            n = iota((BLOCK, SLOTS), 1)
            at_x = lax.rem(xq + step, 4)
            early = ((l + (m >> 5)) & 3) * BLOCK + (m & 31)
            late = ((l + ((m - 128) >> 2)) & 3) * BLOCK + 32 + (m & 3)
            origin = jnp.where(m < 128, early, late) + at_x * 36
            pick = jnp.where(n == origin, 1.0, 0.0).astype(BF16)
            sp32[block(k)] = jnp.dot(pick, source[...], preferred_element_type=F32)
        target[...] = sp32[...].T.astype(BF16)
        if last is not None:
            last[...] = sp32[block(3)].T.astype(BF16)

    tables = selectors(meta_c, 0, False)
    to_f = []
    ag_f = Gather(x_f, sa_f)
    ag_b = Gather(x_b, sa_b)
    ag_m = Gather(x_m, sa_m)

    @pl.when(stream_f.at_first)
    def _():
        stream_b.along_y()

    for q in (0, 1):
        stream_f.arrived(q)
        chosen_rows(tables, q, hop_f, sa_f, sl_f)
        to_f.append(exchange(q, sa_f, sl_f, x_f, lr_f))
        ag_f.start(0, q)

    @pl.when(jnp.logical_not(stream_f.at_first))
    def _():
        stream_f.along_y()

        @pl.when(jnp.logical_not(stream_b.at_first))
        def _():
            stream_b.along_y()

    tables = selectors(meta_c, 16, True)
    for q in (0, 1):
        stream_b.arrived(q)
        chosen_rows(tables, q, hop_b, sa_b, sl_b)
        ag_b.start(0, q)

    ag_f.forward(0)
    to_b = []
    for q in (0, 1):
        arrived(to_f[q])
        spread_last(q, lr_f, x_f)
        ag_f.start(1, q)
        to_b.append(exchange(q, sa_b, sl_b, x_b, lr_b))
    mirror_meta = remote(meta_c, meta_m, mirror)
    mirror_rows = [remote(hop_b.at[:, cols_of(q)], hop_m.at[:, cols_of(q)], mirror) for q in (0, 1)]
    ag_b.forward(0)

    for copy in weights:
        copy.wait()
    for copy in weights_other:
        copy.wait_recv()

    def blocks(k, n):
        return slice(k * BLOCK, (k + n) * BLOCK)

    def project(k, n):
        rows = blocks(k, n)
        pre[rows] = jnp.dot(x_f[rows], win[...], preferred_element_type=F32)
        return remote(pre.at[rows, 2 * HID:4 * HID], pre_r.at[rows], partner)

    def activate(k, n, copy):
        rows = blocks(k, n)
        copy.wait_recv()
        gate = pre[rows, 0:HID] + pre_r[rows, 0:HID]
        up = pre[rows, HID:2 * HID] + pre_r[rows, HID:2 * HID]
        hid[rows, 0:HID] = (gate / (1.0 + jnp.exp(-gate)) * up).astype(BF16)
        return remote(hid.at[rows, 0:HID], hid.at[rows, HID:2 * HID], partner)

    def down(k, n):
        rows = blocks(k, n)

        @pl.loop(0, 7)
        def _(t):
            cols = pl.ds(pl.multiple_of(t * 256, 256), 256)
            got = jnp.dot(hid[rows], wd[:, cols], preferred_element_type=F32)
            po32[rows, cols] = got
            po[rows, cols] = got.astype(BF16)

    pre_0 = project(0, 1)
    ag_f.forward(1)
    hid_0 = activate(0, 1, pre_0)
    stash_own.wait()
    stash_other.wait_recv()
    permuted(st, spt)

    for q in (0, 1):
        arrived(to_b[q])
        spread_last(q, lr_b, x_b)
        ag_b.start(1, q)

    ag_f.near()
    pre_1 = project(1, 2)
    ag_f.far()
    pre_3 = project(3, 1)
    hid_1 = activate(1, 2, pre_1)
    hid_3 = activate(3, 1, pre_3)
    hid_3.wait_recv()
    down(3, 1)
    opp_a = remote(po.at[block(3), A], r_opp_l, right)
    opp_b = remote(po.at[block(3), B], r_opp_r, left)
    hid_1.wait_recv()
    down(1, 2)
    to_left_a = remote(po.at[block(1), A], r_r.at[:, A], left)
    to_right_b = remote(po.at[block(2), B], r_l.at[:, B], right)

    mirror_meta.wait_recv()
    tables = selectors(meta_m, 16, True)
    to_m = []
    for q in (0, 1):
        mirror_rows[q].wait_recv()
        chosen_rows(tables, q, hop_m, sa_m, sl_m)
        to_m.append(exchange(q, sa_m, sl_m, x_m, lr_m))
        ag_m.start(0, q)

    mirror_stash = remote(stash_ref.at[0], stm.at[:, 0:HID], mirror)
    opp_a.wait_recv()
    acc_r[...] = (po32[block(2), A] + r_opp_l[...].astype(F32)).astype(BF16)
    to_right_a = remote(acc_r, r_l.at[:, A], right)
    opp_b.wait_recv()
    acc_l[...] = (po32[block(1), B] + r_opp_r[...].astype(F32)).astype(BF16)
    to_left_b = remote(acc_l, r_r.at[:, B], left)
    ag_b.forward(1)


    hid_0.wait_recv()
    down(0, 1)

    to_r = []
    m = iota((64, 16), 0)
    n = iota((64, 16), 1)
    place = (m >> 4) * 4 + (m & 3)
    packs = [jnp.where((n == place) & (((m >> 2) & 3) == k), 1.0, 0.0).astype(BF16) for k in range(4)]
    for q, waited in ((0, (to_left_a, to_right_a)), (1, (to_right_b, to_left_b))):
        for copy in waited:
            copy.wait_recv()
        total = po32[block(0), cols_of(q)] + r_l[:, cols_of(q)].astype(F32) + r_r[:, cols_of(q)].astype(F32)
        ret[:, cols_of(q)] = total.astype(BF16)
        for t in range(2):
            total = None
            for k in range(4):
                if t * 128 < piece_width(k):
                    low = q * QUART + k * PIECE + t * 128
                    got = jnp.dot(packs[k], ret[128:BLOCK, low:low + 128], preferred_element_type=F32)
                    total = got if total is None else total + got
            ret_l[:, q * PIECE + t * 128:q * PIECE + (t + 1) * 128] = total.astype(BF16)
        to_r.append(exchange_back(q, ret, ret_l, rows_r, lr_r))

    ag_m.forward(0)
    for q in (0, 1):
        arrived(to_m[q])
        spread_last(q, lr_m, x_m)
        ag_m.start(1, q)
    ag_m.forward(1)
    mirror_stash.wait_recv()
    stash_pass = remote(stm.at[:, 0:HID], stm.at[:, HID:2 * HID], partner)

    ag_b.near()
    ag_b.far()

    @pl.loop(0, 7)
    def _(t):
        cols = pl.ds(pl.multiple_of(t * 256, 256), 256)
        own_g[:, cols] = jnp.dot(spt[...], x_b[:, cols], preferred_element_type=F32).astype(BF16)

    stash_pass.wait_recv()
    permuted(stm, spmt, spm_last)
    gates = [meta_c[8 + e:9 + e, 0:64] for e in range(EXPERTS)]
    table = [v * w for v, w in zip(first_slots(meta_c, 0), gates)]
    late = last_slots(meta_c, 0, 16)
    row = iota((16, 64), 0) >> 2
    tail = None
    for e in range(EXPERTS):
        part = jnp.where(row == e, late[e] * gates[e], 0.0)
        tail = part if tail is None else tail + part
    table = jnp.concatenate(table + [tail], axis=0).T
    table_hi = table.astype(BF16)
    table_lo = (table - table_hi.astype(F32)).astype(BF16)
    theirs = pl.ds(pl.multiple_of((1 - c) * TOK, TOK), TOK)
    moe_other = []
    moe_own = []
    for q in (0, 1):
        arrived(to_r[q])
        spread_last(q, lr_r, rows_r)
        got = jnp.dot(table_hi, rows_r[:, cols_of(q)], preferred_element_type=F32)
        got += jnp.dot(table_lo, rows_r[:, cols_of(q)], preferred_element_type=F32)
        mo[:, cols_of(q)] = got.astype(BF16)
        moe_other.append(remote(mo.at[theirs, cols_of(q)], moe_ref.at[0, :, quarter_of(c, q)], partner))
        moe_own.append(here(mo.at[mine, cols_of(q)], moe_ref.at[0, :, quarter_of(c, q)]))

    ag_m.near()

    @pl.loop(0, 7)
    def _(t):
        cols = pl.ds(pl.multiple_of(t * 256, 256), 256)
        po32[0:256, cols] = jnp.dot(
            spmt[:, 0:3 * BLOCK], x_m[0:3 * BLOCK, cols], preferred_element_type=F32
        )

    grads = []
    for q in (0, 1):
        ag_m.far(q)

        @pl.loop(0, 7)
        def _(t):
            cols = pl.ds(pl.multiple_of(q * QUART + t * 128, 128), 128)
            other = jnp.dot(spm_last[...], x_m[block(3), cols], preferred_element_type=F32)
            other = (po32[0:256, cols] + other).astype(BF16)
            g[:, cols] = (own_g[:, cols].astype(F32) + other.astype(F32)).astype(BF16)

        there = grad_ref.at[0, :, quarter_of(c, q)]
        grads.append((remote(g.at[HID:2 * HID, cols_of(q)], there, partner), here(g.at[0:HID, cols_of(q)], there)))

    for copy in moe_own:
        copy.wait()
    for copy in moe_other:
        copy.wait_recv()
    for other, own in grads:
        own.wait()
        other.wait_recv()
    for copy in sent:
        copy.wait_send()
    stream_f.finish()
    stream_b.finish()


def write(moe_ref, grad_ref, moe_out, grad_out, moe, grad, sems):
    pieces = [(moe_ref, moe, moe_out)]
    for k in range(4):
        rows = slice(k * 32, (k + 1) * 32)
        pieces.append((grad_ref.at[:, rows], grad.at[:, rows], grad_out.at[:, rows]))
    loads = [pltpu.make_async_copy(src, held, sems.at[k]) for k, (src, held, _) in enumerate(pieces)]
    for copy in loads:
        copy.start()
    stores = [pltpu.make_async_copy(held, dst, sems.at[k]) for k, (_, held, dst) in enumerate(pieces)]
    for load, store in zip(loads, stores):
        load.wait()
        store.start()
    for store in stores:
        store.wait()


def shards(act_fwd, cot_bwd, routes_fwd, gates_fwd, routes_bwd, gates_bwd, w_in, w_down, stash):
    V = pltpu.VMEM
    scratch = [
        V((2, TOK), jnp.int32), V((2, TOK), F32), V((2, TOK), jnp.int32), V((2, TOK), F32),
        V((32, 128), F32), V((32, 128), F32), V((32, 128), F32), V((32, 128), F32),
        V((64, HALF), BF16), V((64, HALF), BF16), V((64, HALF), BF16),
        V((TOK, QUART), BF16), V((TOK, QUART), BF16), V((TOK, QUART), BF16), V((TOK, QUART), BF16),
        V((128, HALF), BF16), V((128, HALF), BF16), V((128, HALF), BF16),
        V((64, 2 * PIECE), BF16), V((64, 2 * PIECE), BF16), V((64, 2 * PIECE), BF16),
        V((64, 2 * PIECE), BF16), V((64, 2 * PIECE), BF16), V((64, 2 * PIECE), BF16), V((64, 2 * PIECE), BF16),
        V((SLOTS, HALF), BF16), V((SLOTS, HALF), BF16), V((SLOTS, HALF), BF16),
        V((HALF, 4 * HID), BF16), V((2 * HID, HALF), BF16),
        V((SLOTS, 2 * HID), BF16), V((SLOTS, 2 * HID), BF16),
        V((SLOTS, 2 * HID), F32), V((2 * HID, SLOTS), BF16), V((2 * HID, SLOTS), BF16), V((2 * HID, BLOCK), BF16),
        V((SLOTS, 4 * HID), F32), V((SLOTS, 2 * HID), F32), V((SLOTS, 2 * HID), BF16),
        V((SLOTS, HALF), F32), V((SLOTS, HALF), BF16),
        V((BLOCK, QUART), BF16), V((BLOCK, QUART), BF16), V((BLOCK, QUART), BF16), V((BLOCK, QUART), BF16),
        V((BLOCK, HALF), BF16), V((BLOCK, HALF), BF16),
        V((BLOCK, HALF), BF16), V((64, 2 * PIECE), BF16), V((BLOCK, HALF), BF16),
        V((64, HALF), BF16), V((2 * HID, HALF), BF16), V((2 * HID, HALF), BF16),
        pltpu.SemaphoreType.DMA((128,)), pltpu.SemaphoreType.DMA((128,)), pltpu.SemaphoreType.DMA((32,)),
        pltpu.SemaphoreType.DMA((12,)), pltpu.SemaphoreType.DMA((12,)),
        pltpu.SemaphoreType.DMA((4,)),
    ]
    hbm = pl.BlockSpec(memory_space=pltpu.HBM)
    results = pl.pallas_call(
        kernel,
        out_shape=(
            jax.ShapeDtypeStruct((1, TOK, D), BF16),
            jax.ShapeDtypeStruct((1, HID, D), BF16),
        ),
        in_specs=[hbm] * 9,
        out_specs=(hbm, hbm),
        scratch_shapes=scratch,
        compiler_params=pltpu.CompilerParams(
            collective_id=0, has_side_effects=True, vmem_limit_bytes=56 * 1024 * 1024
        ),
    )(
        routes_fwd[0].T, gates_fwd[0].T, routes_bwd[0].T, gates_bwd[0].T,
        act_fwd, cot_bwd, w_in, w_down, stash,
    )
    return pl.pallas_call(
        write,
        out_shape=tuple(jax.ShapeDtypeStruct(r.shape, r.dtype) for r in results),
        in_specs=[hbm, hbm],
        out_specs=(hbm, hbm),
        scratch_shapes=[
            pltpu.VMEM((1, TOK, D), BF16), pltpu.VMEM((1, HID, D), BF16), pltpu.SemaphoreType.DMA((6,)),
        ],
    )(*results)


def solution(mesh):
    rows = P("pipe", "expert", None)
    in_specs = (rows, rows, rows, rows, rows, rows, P("pipe", None, None, "expert"), rows, rows)
    return jax.shard_map(shards, mesh=mesh, in_specs=in_specs, out_specs=(rows, rows), check_vma=False)
```

```python
import jax
import jax.numpy as jnp
from jax import lax
from jax.experimental import pallas as pl
from jax.experimental.pallas import tpu as pltpu
from jax.sharding import PartitionSpec as P

MESH = pl.DeviceIdType.MESH
EXPERTS = 4
CAP = 18
TOK = 32
D = 3584
HALF = 1792
QUART = 896
HID = 128
SLOTS = 576
BLOCK = 144
PIECE = 256
F32 = jnp.float32
BF16 = jnp.bfloat16


def iota(shape, axis):
    return lax.broadcasted_iota(jnp.int32, shape, axis)


def piece_width(k):
    return min(PIECE, QUART - k * PIECE)


def kernel(
    route_f_ref, gate_f_ref, route_b_ref, gate_b_ref, act_ref, cot_ref, win_ref, wdn_ref, stash_ref,
    moe_ref, grad_ref,
    route_f, gate_f, route_b, gate_b, meta_o, meta_p, meta_c, meta_m,
    hop_f, hop_b, hop_m, via_f1, via_f2, via_b1, via_b2,
    sa_f, sa_b, sa_m, sl_f, sl_b, sl_m,
    lr_f, lr_b, lr_m, lr_r,
    x_f, x_b, x_m,
    win, wd, st, stm, sp32, spt, spmt, spm_last,
    pre, pre_r, hid,
    po32, po, r_opp_l, r_opp_r, acc_r, acc_l, r_l, r_r,
    ret, ret_l, rows_r, mo, own_g, g,
    send_sem, recv_sem, local_sem, hop_send, hop_recv, small_sem,
):
    p = lax.axis_index("pipe")
    i = lax.axis_index("expert")
    n_pipe = lax.axis_size("pipe")
    c = lax.rem(i, 2)
    xq = lax.rem(lax.div(i, 2), 4)
    l = lax.div(i, 8)

    def at(pp, ll, xx, cc):
        return (pp, ll * 8 + xx * 2 + cc)

    y = lax.rem(p, 4)
    zh = lax.div(p, 4)
    n_zh = n_pipe // 4

    def section(yy, up):
        return lax.rem(zh + n_zh + up, n_zh) * 4 + yy

    mirror = at(n_pipe - 1 - p, l, xq, c)
    partner = at(p, l, xq, 1 - c)
    right = at(p, l, lax.rem(xq + 1, 4), c)
    left = at(p, l, lax.rem(xq + 3, 4), c)

    def zdev(d):
        return lax.rem(l + d, 4)

    small = [(route_f_ref, route_f), (gate_f_ref, gate_f), (route_b_ref, route_b), (gate_b_ref, gate_b)]
    small = [pltpu.make_async_copy(src, dst, small_sem.at[k]) for k, (src, dst) in enumerate(small)]
    for copy in small:
        copy.start()
    barrier = pltpu.get_barrier_semaphore()
    greeted = [at(section(lax.rem(y + d, 4), 0), l, xq, cc) for d in (1, 2, 3) for cc in (c, 1 - c)]
    greeted += [at(section(y, up), l, xq, cc) for up in (1, -1) for cc in (c, 1 - c)]
    greeted += [at(p, zdev(d), xq, c) for d in (1, 2, 3)]
    greeted += [mirror, partner, right, left]
    for other in greeted:
        pl.semaphore_signal(barrier, inc=1, device_id=other, device_id_type=MESH)

    used = [0, 0]
    sent = []

    def remote(src, dst, device):
        k = used[0]
        used[0] += 1
        copy = pltpu.make_async_remote_copy(
            src_ref=src, dst_ref=dst, send_sem=send_sem.at[k], recv_sem=recv_sem.at[k],
            device_id=device, device_id_type=MESH,
        )
        copy.start()
        sent.append(copy)
        return copy

    def here(src, dst):
        k = used[1]
        used[1] += 1
        copy = pltpu.make_async_copy(src, dst, local_sem.at[k])
        copy.start()
        return copy

    def half_of(core):
        return pl.ds(pl.multiple_of(core * HALF, HALF), HALF)

    def quarter_of(core, q):
        return pl.ds(pl.multiple_of(core * HALF + q * QUART, 128), QUART)

    def cols_of(q):
        return slice(q * QUART, (q + 1) * QUART)

    A = cols_of(0)
    B = cols_of(1)
    mine = pl.ds(pl.multiple_of(c * TOK, TOK), TOK)

    def table_rows(routes, gates, row):
        e = iota((8, TOK), 0)
        first = routes[0:1] == e
        second = routes[1:2] == e
        hits = jnp.where(first | second, 1.0, 0.0).astype(F32)
        weight = jnp.where(first, gates[0:1], 0.0) + jnp.where(second, gates[1:2], 0.0)
        t = iota((TOK, 128), 0)
        lane = iota((TOK, 128), 1) - c * TOK
        upto = jnp.where((t <= lane) & (lane < TOK), 1.0, 0.0).astype(F32)
        place = jnp.where(t == lane, 1.0, 0.0).astype(F32)
        count = jnp.dot(hits, upto, preferred_element_type=F32)
        placed = jnp.dot(hits, place, preferred_element_type=F32)
        meta_o[row:row + 8] = count * placed
        meta_o[row + 8:row + 16] = jnp.dot(
            weight, place, precision=lax.Precision.HIGHEST, preferred_element_type=F32
        )

    pl.semaphore_wait(barrier, len(greeted))

    def hop(k, src, dst, device, base):
        return pltpu.make_async_remote_copy(
            src_ref=src, dst_ref=dst, send_sem=hop_send.at[base + k], recv_sem=hop_recv.at[base + k],
            device_id=device, device_id_type=MESH,
        )

    class Stream:
        def __init__(self, src, rows, via_1, via_2, base, first, up, column):
            self.src, self.rows, self.via_1, self.via_2, self.base = src, rows, via_1, via_2, base
            self.up, self.column, self.ahead = up, column, up
            self.first = first
            self.last = 3 - first
            self.at_first = y == first
            self.at_last = y == self.last

        def piece(self, k):
            return self.src.at[0, :, pl.ds(pl.multiple_of(k * QUART, 128), QUART)]

        def final(self, src, core, q, device):
            cols = pl.ds(pl.multiple_of(q * QUART, 128), QUART)
            return hop(2 * q + lax.rem(c + core, 2), src, self.rows.at[mine, cols], device, self.base)

        def start(self):
            @pl.when(jnp.logical_not(self.at_last))
            def _():
                for q in (0, 1):
                    for d in (0, 1):
                        core = lax.rem(c + d, 2)
                        device = at(section(y + self.ahead, 0), l, xq, core)
                        self.final(self.piece(2 * core + q), core, q, device).start()

            @pl.when(self.at_last)
            def _():
                hop(5, self.piece(3), self.via_2, at(section(y, self.up), l, xq, c), self.base).start()
                for k in (1, 2, 0):
                    device = at(section(self.column(k), 0), l, xq, c)
                    pltpu.make_async_remote_copy(
                        src_ref=self.piece(k), dst_ref=self.via_1,
                        send_sem=hop_send.at[self.base + k], recv_sem=hop_recv.at[self.base + 4],
                        device_id=device, device_id_type=MESH,
                    ).start()

        def along_z(self):
            @pl.when(jnp.logical_not(self.at_last))
            def _():
                self.wait(4, self.via_1)

                @pl.when(self.at_first)
                def _():
                    device = at(section(y, self.up), l, xq, 0)
                    hop_to = self.rows.at[mine, A]
                    pltpu.make_async_remote_copy(
                        src_ref=self.via_1, dst_ref=hop_to, send_sem=hop_send.at[self.base + 5],
                        recv_sem=hop_recv.at[self.base + c],
                        device_id=device, device_id_type=MESH,
                    ).start()

                @pl.when(jnp.logical_not(self.at_first))
                def _():
                    hop(5, self.via_1, self.via_2, at(section(y, self.up), l, xq, c), self.base).start()

        def along_y(self):
            k = self.column(y)
            core = lax.div(k, 2)
            q = lax.rem(k, 2)
            self.wait(5, self.via_2)
            cols = pl.ds(pl.multiple_of(q * QUART, 128), QUART)
            pltpu.make_async_remote_copy(
                src_ref=self.via_2, dst_ref=self.rows.at[mine, cols], send_sem=hop_send.at[self.base + 4],
                recv_sem=hop_recv.at[self.base + 2 * q + lax.rem(c + core, 2)],
                device_id=at(section(self.first, 0), l, xq, core), device_id_type=MESH,
            ).start()

        def wait(self, k, ref):
            hop(k, ref, ref, partner, self.base).wait_recv()

        def arrived(self, q):
            for d in (0, 1):
                hop(2 * q + d, self.rows.at[mine, cols_of(q)], self.rows.at[mine, cols_of(q)], partner, self.base).wait_recv()

        def finish(self):
            for k in (0, 1, 2, 5):
                hop(k, self.via_1, self.via_1, partner, self.base).wait_send()

            @pl.when(jnp.logical_not(self.at_last))
            def _():
                hop(3, self.via_1, self.via_1, partner, self.base).wait_send()

            @pl.when(jnp.logical_not(self.at_first))
            def _():
                hop(4, self.via_2, self.via_2, partner, self.base).wait_send()

    stream_f = Stream(act_ref, hop_f, via_f1, via_f2, 0, 0, 1, lambda v: v)
    stream_b = Stream(cot_ref, hop_b, via_b1, via_b2, 6, 3, -1, lambda v: 3 - v)
    stream_f.start()
    stream_b.start()
    for copy in small:
        copy.wait()
    table_rows(route_f, gate_f, 0)
    table_rows(route_b, gate_b, 16)
    weights = []
    for s in (0, 1):
        weights.append(here(win_ref.at[0, s, half_of(c)], win.at[:, s * HID:(s + 1) * HID]))
    weights.append(here(wdn_ref.at[0, :, half_of(c)], wd.at[0:HID]))
    stash_own = here(stash_ref.at[0], st.at[:, 0:HID])
    meta_copy = remote(meta_o, meta_p, partner)
    weights_other = []
    for s in (0, 1):
        weights_other.append(
            remote(win_ref.at[0, s, half_of(1 - c)], win.at[:, (2 + s) * HID:(3 + s) * HID], partner)
        )
    weights_other.append(remote(wdn_ref.at[0, :, half_of(1 - c)], wd.at[HID:2 * HID], partner))
    stash_other = remote(stash_ref.at[0], st.at[:, HID:2 * HID], partner)

    stream_f.along_z()
    stream_b.along_z()

    meta_copy.wait_recv()
    meta_c[...] = meta_o[...] + meta_p[...]

    def first_slots(meta, row):
        j = iota((32, 64), 0)
        lane = iota((32, 64), 1)
        core = (j >= CAP).astype(jnp.int32)
        wanted = (j - CAP * core + 1).astype(F32)
        same = (lane >= TOK).astype(jnp.int32) == core
        return [
            jnp.where((meta[row + e:row + e + 1, 0:64] == wanted) & same, 1.0, 0.0).astype(F32)
            for e in range(EXPERTS)
        ]

    def last_slots(meta, row, rows):
        r = iota((rows, 64), 0)
        lane = iota((rows, 64), 1)
        wanted = ((r & 3) + (32 - CAP + 1)).astype(F32)
        return [
            jnp.where((meta[row + e:row + e + 1, 0:64] == wanted) & (lane >= TOK), 1.0, 0.0).astype(F32)
            for e in range(EXPERTS)
        ]

    def selectors(meta, row, weigh):
        a = first_slots(meta, row)
        b = last_slots(meta, row, 16)
        sel_a = jnp.concatenate(a, axis=0)
        sel_b = jnp.concatenate(b, axis=0)
        gate_a = gate_b = None
        if weigh:
            gates = [meta[row + 8 + e:row + 9 + e, 0:64] for e in range(EXPERTS)]
            gate_a = jnp.sum(jnp.concatenate([v * w for v, w in zip(a, gates)], axis=0), axis=1, keepdims=True)
            gate_b = jnp.sum(jnp.concatenate([v * w for v, w in zip(b, gates)], axis=0), axis=1, keepdims=True)
        piece = (iota((64, 64), 0) >> 2) & 3
        parts = [jnp.where(piece == k, sel_b, 0.0).astype(BF16) for k in range(4)]
        return sel_a.astype(BF16), parts, gate_a, gate_b

    def chosen_rows(tables, q, hop, sa, sl):
        sel_a, parts, gate_a, gate_b = tables
        got = jnp.dot(sel_a, hop[:, cols_of(q)], preferred_element_type=F32)
        if gate_a is not None:
            got = got * gate_a
        sa[:, cols_of(q)] = got.astype(BF16)
        for t in range(2):
            total = None
            for k in range(4):
                if t * 128 < piece_width(k):
                    low = q * QUART + k * PIECE + t * 128
                    got = jnp.dot(parts[k], hop[:, low:low + 128], preferred_element_type=F32)
                    total = got if total is None else total + got
            if gate_b is not None:
                total = total * gate_b
            sl[:, q * PIECE + t * 128:q * PIECE + (t + 1) * 128] = total.astype(BF16)

    rows_here = pl.ds(pl.multiple_of(l * 32, 32), 32)
    last_here = pl.ds(pl.multiple_of(l * 16, 16), 16)

    def last_cols(q):
        return slice(q * PIECE, (q + 1) * PIECE)

    def exchange(q, sa, sl, rows, last):
        out = []
        for d in (2, 1, 3):
            e = zdev(d)
            device = at(p, e, xq, c)
            k = 4 - d
            theirs = pl.ds(pl.multiple_of(e * 32, 32), 32)
            last_theirs = pl.ds(pl.multiple_of(e * 16, 16), 16)
            out.append(remote(sa.at[theirs, cols_of(q)], rows.at[k * 32:(k + 1) * 32, cols_of(q)], device))
            out.append(remote(sl.at[last_theirs, last_cols(q)], last.at[k * 16:(k + 1) * 16, last_cols(q)], device))
        own = [
            here(sa.at[rows_here, cols_of(q)], rows.at[0:32, cols_of(q)]),
            here(sl.at[last_here, last_cols(q)], last.at[0:16, last_cols(q)]),
        ]
        return out, own

    def exchange_back(q, rows, last, back, back_last):
        out = []
        for d in (2, 1, 3):
            device = at(p, zdev(d), xq, c)
            out.append(remote(rows.at[d * 32:(d + 1) * 32, cols_of(q)], back.at[rows_here, cols_of(q)], device))
            out.append(remote(last.at[d * 16:(d + 1) * 16, last_cols(q)], back_last.at[last_here, last_cols(q)], device))
        own = [
            here(rows.at[0:32, cols_of(q)], back.at[rows_here, cols_of(q)]),
            here(last.at[0:16, last_cols(q)], back_last.at[last_here, last_cols(q)]),
        ]
        return out, own

    def arrived(copies):
        for copy in copies[0]:
            copy.wait_recv()
        for copy in copies[1]:
            copy.wait()

    def spread_last(q, last, rows):
        m = iota((16, 64), 0)
        n = iota((16, 64), 1)
        for k in range(4):
            width = piece_width(k)
            place = (m >> 2) * 16 + 4 * k + (m & 3)
            pick = jnp.where(n == place, 1.0, 0.0).astype(BF16)
            got = jnp.dot(pick, last[:, q * PIECE:q * PIECE + width], preferred_element_type=F32)
            low = q * QUART + k * PIECE
            rows[128:BLOCK, low:low + width] = got.astype(BF16)

    def block(k):
        return slice(k * BLOCK, (k + 1) * BLOCK)

    def part(k, n):
        return slice(k * BLOCK, k * BLOCK + 32) if n == 0 else slice(k * BLOCK + 32, (k + 1) * BLOCK)

    class Gather:
        def __init__(self, x, sa):
            self.x, self.sa = x, sa
            self.copies = {}

        def start(self, n, q):
            x = self.x
            src = self.sa.at[rows_here, cols_of(q)] if n == 0 else x.at[part(0, 1), cols_of(q)]
            sides = [(1, right), (2, left)]
            for k, device in sides if q == 0 else sides[::-1]:
                self.copies[n, q, k] = remote(src, x.at[part(k, n), cols_of(q)], device)

        def forward(self, n):
            x = self.x
            for q, k, device in ((0, 1, right), (1, 2, left)):
                self.copies[n, q, k].wait_recv()
                self.copies[n, q, 3] = remote(x.at[part(k, n), cols_of(q)], x.at[part(3, n), cols_of(q)], device)

        def near(self):
            for n in (0, 1):
                self.copies[n, 0, 2].wait_recv()
                self.copies[n, 1, 1].wait_recv()

        def far(self, *halves):
            for q in halves or (0, 1):
                self.copies[0, q, 3].wait_recv()
                self.copies[1, q, 3].wait_recv()

    def permuted(source, target, last=None):
        for k, step in enumerate((0, 3, 1, 2)):
            m = iota((BLOCK, SLOTS), 0)
            n = iota((BLOCK, SLOTS), 1)
            at_x = lax.rem(xq + step, 4)
            early = ((l + (m >> 5)) & 3) * BLOCK + (m & 31)
            late = ((l + ((m - 128) >> 2)) & 3) * BLOCK + 32 + (m & 3)
            origin = jnp.where(m < 128, early, late) + at_x * 36
            pick = jnp.where(n == origin, 1.0, 0.0).astype(BF16)
            sp32[block(k)] = jnp.dot(pick, source[...], preferred_element_type=F32)
        target[...] = sp32[...].T.astype(BF16)
        if last is not None:
            last[...] = sp32[block(3)].T.astype(BF16)

    tables = selectors(meta_c, 0, False)
    to_f = []
    ag_f = Gather(x_f, sa_f)
    ag_b = Gather(x_b, sa_b)
    ag_m = Gather(x_m, sa_m)

    @pl.when(stream_f.at_first)
    def _():
        stream_b.along_y()

    for q in (0, 1):
        stream_f.arrived(q)
        chosen_rows(tables, q, hop_f, sa_f, sl_f)
        to_f.append(exchange(q, sa_f, sl_f, x_f, lr_f))
        ag_f.start(0, q)

    @pl.when(jnp.logical_not(stream_f.at_first))
    def _():
        stream_f.along_y()

        @pl.when(jnp.logical_not(stream_b.at_first))
        def _():
            stream_b.along_y()

    tables = selectors(meta_c, 16, True)
    for q in (0, 1):
        stream_b.arrived(q)
        chosen_rows(tables, q, hop_b, sa_b, sl_b)
        ag_b.start(0, q)

    ag_f.forward(0)
    to_b = []
    for q in (0, 1):
        arrived(to_f[q])
        spread_last(q, lr_f, x_f)
        ag_f.start(1, q)
        to_b.append(exchange(q, sa_b, sl_b, x_b, lr_b))
    mirror_meta = remote(meta_c, meta_m, mirror)
    mirror_rows = [remote(hop_b.at[:, cols_of(q)], hop_m.at[:, cols_of(q)], mirror) for q in (0, 1)]
    ag_b.forward(0)

    for copy in weights:
        copy.wait()
    for copy in weights_other:
        copy.wait_recv()

    def blocks(k, n):
        return slice(k * BLOCK, (k + n) * BLOCK)

    def project(k, n):
        rows = blocks(k, n)
        pre[rows] = jnp.dot(x_f[rows], win[...], preferred_element_type=F32)
        return remote(pre.at[rows, 2 * HID:4 * HID], pre_r.at[rows], partner)

    def activate(k, n, copy):
        rows = blocks(k, n)
        copy.wait_recv()
        gate = pre[rows, 0:HID] + pre_r[rows, 0:HID]
        up = pre[rows, HID:2 * HID] + pre_r[rows, HID:2 * HID]
        hid[rows, 0:HID] = (gate / (1.0 + jnp.exp(-gate)) * up).astype(BF16)
        return remote(hid.at[rows, 0:HID], hid.at[rows, HID:2 * HID], partner)

    def down(k, n):
        rows = blocks(k, n)

        @pl.loop(0, 7)
        def _(t):
            cols = pl.ds(pl.multiple_of(t * 256, 256), 256)
            got = jnp.dot(hid[rows], wd[:, cols], preferred_element_type=F32)
            po32[rows, cols] = got
            po[rows, cols] = got.astype(BF16)

    pre_0 = project(0, 1)
    ag_f.forward(1)
    hid_0 = activate(0, 1, pre_0)
    stash_own.wait()
    stash_other.wait_recv()
    permuted(st, spt)

    for q in (0, 1):
        arrived(to_b[q])
        spread_last(q, lr_b, x_b)
        ag_b.start(1, q)

    ag_f.near()
    pre_1 = project(1, 2)
    ag_f.far()
    pre_3 = project(3, 1)
    hid_1 = activate(1, 2, pre_1)
    hid_3 = activate(3, 1, pre_3)
    hid_3.wait_recv()
    down(3, 1)
    opp_a = remote(po.at[block(3), A], r_opp_l, right)
    opp_b = remote(po.at[block(3), B], r_opp_r, left)
    hid_1.wait_recv()
    down(1, 2)
    to_left_a = remote(po.at[block(1), A], r_r.at[:, A], left)
    to_right_b = remote(po.at[block(2), B], r_l.at[:, B], right)

    mirror_meta.wait_recv()
    tables = selectors(meta_m, 16, True)
    to_m = []
    for q in (0, 1):
        mirror_rows[q].wait_recv()
        chosen_rows(tables, q, hop_m, sa_m, sl_m)
        to_m.append(exchange(q, sa_m, sl_m, x_m, lr_m))
        ag_m.start(0, q)

    opp_a.wait_recv()
    acc_r[...] = (po32[block(2), A] + r_opp_l[...].astype(F32)).astype(BF16)
    to_right_a = remote(acc_r, r_l.at[:, A], right)
    opp_b.wait_recv()
    acc_l[...] = (po32[block(1), B] + r_opp_r[...].astype(F32)).astype(BF16)
    to_left_b = remote(acc_l, r_r.at[:, B], left)
    mirror_stash = remote(stash_ref.at[0], stm.at[:, 0:HID], mirror)
    ag_b.forward(1)


    hid_0.wait_recv()
    down(0, 1)

    to_r = []
    m = iota((64, 16), 0)
    n = iota((64, 16), 1)
    place = (m >> 4) * 4 + (m & 3)
    packs = [jnp.where((n == place) & (((m >> 2) & 3) == k), 1.0, 0.0).astype(BF16) for k in range(4)]
    for q, waited in ((0, (to_left_a, to_right_a)), (1, (to_right_b, to_left_b))):
        for copy in waited:
            copy.wait_recv()
        total = po32[block(0), cols_of(q)] + r_l[:, cols_of(q)].astype(F32) + r_r[:, cols_of(q)].astype(F32)
        ret[:, cols_of(q)] = total.astype(BF16)
        for t in range(2):
            total = None
            for k in range(4):
                if t * 128 < piece_width(k):
                    low = q * QUART + k * PIECE + t * 128
                    got = jnp.dot(packs[k], ret[128:BLOCK, low:low + 128], preferred_element_type=F32)
                    total = got if total is None else total + got
            ret_l[:, q * PIECE + t * 128:q * PIECE + (t + 1) * 128] = total.astype(BF16)
        to_r.append(exchange_back(q, ret, ret_l, rows_r, lr_r))

    ag_m.forward(0)
    for q in (0, 1):
        arrived(to_m[q])
        spread_last(q, lr_m, x_m)
        ag_m.start(1, q)
    mirror_stash.wait_recv()
    stash_pass = remote(stm.at[:, 0:HID], stm.at[:, HID:2 * HID], partner)

    ag_b.near()
    ag_b.far()

    @pl.loop(0, 7)
    def _(t):
        cols = pl.ds(pl.multiple_of(t * 256, 256), 256)
        own_g[:, cols] = jnp.dot(spt[...], x_b[:, cols], preferred_element_type=F32).astype(BF16)

    stash_pass.wait_recv()
    permuted(stm, spmt, spm_last)
    gates = [meta_c[8 + e:9 + e, 0:64] for e in range(EXPERTS)]
    table = [v * w for v, w in zip(first_slots(meta_c, 0), gates)]
    late = last_slots(meta_c, 0, 16)
    row = iota((16, 64), 0) >> 2
    tail = None
    for e in range(EXPERTS):
        own_part = jnp.where(row == e, late[e] * gates[e], 0.0)
        tail = own_part if tail is None else tail + own_part
    table = jnp.concatenate(table + [tail], axis=0).T
    table_hi = table.astype(BF16)
    table_lo = (table - table_hi.astype(F32)).astype(BF16)
    ag_m.forward(1)
    theirs = pl.ds(pl.multiple_of((1 - c) * TOK, TOK), TOK)
    moe_other = []
    moe_own = []
    for q in (0, 1):
        arrived(to_r[q])
        spread_last(q, lr_r, rows_r)
        got = jnp.dot(table_hi, rows_r[:, cols_of(q)], preferred_element_type=F32)
        got += jnp.dot(table_lo, rows_r[:, cols_of(q)], preferred_element_type=F32)
        mo[:, cols_of(q)] = got.astype(BF16)
        moe_other.append(remote(mo.at[theirs, cols_of(q)], moe_ref.at[0, :, quarter_of(c, q)], partner))
        moe_own.append(here(mo.at[mine, cols_of(q)], moe_ref.at[0, :, quarter_of(c, q)]))

    ag_m.near()

    @pl.loop(0, 7)
    def _(t):
        cols = pl.ds(pl.multiple_of(t * 256, 256), 256)
        po32[0:256, cols] = jnp.dot(
            spmt[:, 0:3 * BLOCK], x_m[0:3 * BLOCK, cols], preferred_element_type=F32
        )

    grads = []
    for q in (0, 1):
        ag_m.far(q)

        @pl.loop(0, 7)
        def _(t):
            cols = pl.ds(pl.multiple_of(q * QUART + t * 128, 128), 128)
            other = jnp.dot(spm_last[...], x_m[block(3), cols], preferred_element_type=F32)
            other = (po32[0:256, cols] + other).astype(BF16)
            g[:, cols] = (own_g[:, cols].astype(F32) + other.astype(F32)).astype(BF16)

        there = grad_ref.at[0, :, quarter_of(c, q)]
        grads.append((remote(g.at[HID:2 * HID, cols_of(q)], there, partner), here(g.at[0:HID, cols_of(q)], there)))

    for copy in moe_own:
        copy.wait()
    for copy in moe_other:
        copy.wait_recv()
    for other, own in grads:
        own.wait()
        other.wait_recv()
    for copy in sent:
        copy.wait_send()
    stream_f.finish()
    stream_b.finish()


def write(moe_ref, grad_ref, moe_out, grad_out, moe, grad, sems):
    pieces = [(moe_ref, moe, moe_out)]
    for k in range(4):
        rows = slice(k * 32, (k + 1) * 32)
        pieces.append((grad_ref.at[:, rows], grad.at[:, rows], grad_out.at[:, rows]))
    loads = [pltpu.make_async_copy(src, held, sems.at[k]) for k, (src, held, _) in enumerate(pieces)]
    for copy in loads:
        copy.start()
    stores = [pltpu.make_async_copy(held, dst, sems.at[k]) for k, (_, held, dst) in enumerate(pieces)]
    for load, store in zip(loads, stores):
        load.wait()
        store.start()
    for store in stores:
        store.wait()


def shards(act_fwd, cot_bwd, routes_fwd, gates_fwd, routes_bwd, gates_bwd, w_in, w_down, stash):
    V = pltpu.VMEM
    scratch = [
        V((2, TOK), jnp.int32), V((2, TOK), F32), V((2, TOK), jnp.int32), V((2, TOK), F32),
        V((32, 128), F32), V((32, 128), F32), V((32, 128), F32), V((32, 128), F32),
        V((64, HALF), BF16), V((64, HALF), BF16), V((64, HALF), BF16),
        V((TOK, QUART), BF16), V((TOK, QUART), BF16), V((TOK, QUART), BF16), V((TOK, QUART), BF16),
        V((128, HALF), BF16), V((128, HALF), BF16), V((128, HALF), BF16),
        V((64, 2 * PIECE), BF16), V((64, 2 * PIECE), BF16), V((64, 2 * PIECE), BF16),
        V((64, 2 * PIECE), BF16), V((64, 2 * PIECE), BF16), V((64, 2 * PIECE), BF16), V((64, 2 * PIECE), BF16),
        V((SLOTS, HALF), BF16), V((SLOTS, HALF), BF16), V((SLOTS, HALF), BF16),
        V((HALF, 4 * HID), BF16), V((2 * HID, HALF), BF16),
        V((SLOTS, 2 * HID), BF16), V((SLOTS, 2 * HID), BF16),
        V((SLOTS, 2 * HID), F32), V((2 * HID, SLOTS), BF16), V((2 * HID, SLOTS), BF16), V((2 * HID, BLOCK), BF16),
        V((SLOTS, 4 * HID), F32), V((SLOTS, 2 * HID), F32), V((SLOTS, 2 * HID), BF16),
        V((SLOTS, HALF), F32), V((SLOTS, HALF), BF16),
        V((BLOCK, QUART), BF16), V((BLOCK, QUART), BF16), V((BLOCK, QUART), BF16), V((BLOCK, QUART), BF16),
        V((BLOCK, HALF), BF16), V((BLOCK, HALF), BF16),
        V((BLOCK, HALF), BF16), V((64, 2 * PIECE), BF16), V((BLOCK, HALF), BF16),
        V((64, HALF), BF16), V((2 * HID, HALF), BF16), V((2 * HID, HALF), BF16),
        pltpu.SemaphoreType.DMA((128,)), pltpu.SemaphoreType.DMA((128,)), pltpu.SemaphoreType.DMA((32,)),
        pltpu.SemaphoreType.DMA((12,)), pltpu.SemaphoreType.DMA((12,)),
        pltpu.SemaphoreType.DMA((4,)),
    ]
    hbm = pl.BlockSpec(memory_space=pltpu.HBM)
    results = pl.pallas_call(
        kernel,
        out_shape=(
            jax.ShapeDtypeStruct((1, TOK, D), BF16),
            jax.ShapeDtypeStruct((1, HID, D), BF16),
        ),
        in_specs=[hbm] * 9,
        out_specs=(hbm, hbm),
        scratch_shapes=scratch,
        compiler_params=pltpu.CompilerParams(
            collective_id=0, has_side_effects=True, vmem_limit_bytes=56 * 1024 * 1024
        ),
    )(
        routes_fwd[0].T, gates_fwd[0].T, routes_bwd[0].T, gates_bwd[0].T,
        act_fwd, cot_bwd, w_in, w_down, stash,
    )
    return pl.pallas_call(
        write,
        out_shape=tuple(jax.ShapeDtypeStruct(r.shape, r.dtype) for r in results),
        in_specs=[hbm, hbm],
        out_specs=(hbm, hbm),
        scratch_shapes=[
            pltpu.VMEM((1, TOK, D), BF16), pltpu.VMEM((1, HID, D), BF16), pltpu.SemaphoreType.DMA((6,)),
        ],
    )(*results)


def solution(mesh):
    rows = P("pipe", "expert", None)
    in_specs = (rows, rows, rows, rows, rows, rows, P("pipe", None, None, "expert"), rows, rows)
    return jax.shard_map(shards, mesh=mesh, in_specs=in_specs, out_specs=(rows, rows), check_vma=False)
```
